256 devices in a mesh: row: 16 (over z, x_lo), col: 16 (over y, x_hi, core).
Axes of the slice: x: 4 (x_hi: 2, x_lo: 2; x = x_hi * 2 + x_lo), y: 4, z: 8, core: 2. Of those that a mesh axis runs over, the one named last changes fastest.
Arguments:
- tiles: bfloat16 [16, 16, 320, 128, 128], P('row', 'col'), may hold values from 0 to 0.099609375
- tile_rows: int32 [16, 16, 320], P('row', 'col'), may hold values from 0 to 63
- tile_cols: int32 [16, 16, 320], P('row', 'col'), may hold values from 0 to 63
- node_level: int32 [131072], P(('row', 'col')), may hold values from 0 to 127
- level_scale: float32 [128], replicated, may hold values from 0.15 to 1.5
- stored_basis: bfloat16 [131072, 64], P(('row', 'col')), may hold values from -20 to 20
- start_block: bfloat16 [131072, 32], P(('row', 'col')), may hold values from -33 to 33
Outputs:
- first_block: bfloat16 [131072, 32], P(('row', 'col'))
- second_block: bfloat16 [131072, 32], P(('row', 'col'))
The draws below stay inside these ranges and needn't reach their ends.
All inputs are finite; a program needn't handle non-finite values.
Results may differ from the reference program's by a relative error of at most 0.02.
Values may be sent and summed in bfloat16 or wider, within the bound.
No kernel may reach another device: no remote copies, remote signals or barrier semaphores. Data moves between devices by JAX's collectives and lax.ppermute only.
A program may use at most 64 MiB of HBM per device.

```python
import math
import jax
import jax.numpy as jnp
from jax import lax

NODE_DEV = 512
TILES_DEV = 320
TILE = 128
BLOCK = 32
STORED = 64
LEVELS = 128
NODES = 131072
N_ROW = 16
N_COL = 16


def shared_levels(key):
    return jax.random.randint(jax.random.fold_in(key, 101), (NODES,), 0, LEVELS)


def shared_basis(key):
    levels = shared_levels(key)
    gauss = jnp.clip(jax.random.normal(jax.random.fold_in(key, 102), (NODES, STORED), jnp.float32), -5.0, 5.0)
    noise = gauss
    groups = levels // (LEVELS // STORED)
    member = (groups[:, None] == jnp.arange(STORED)[None, :]).astype(jnp.float32)
    col_scale = jnp.exp(jax.random.uniform(jax.random.fold_in(key, 104), (STORED,), jnp.float32, 0.0, math.log(3.0)))
    return noise * (0.3 + member) * col_scale[None, :]


def draw_node_level(key, part):
    return shared_levels(key).astype(jnp.int32)


def draw_stored_basis(key, part):
    basis = shared_basis(key)
    return basis.astype(jnp.bfloat16)


def draw_start_block(key, part):
    basis = shared_basis(key)
    key = jax.random.fold_in(key, 3)
    mixing = jax.random.uniform(jax.random.fold_in(key, 1), (2, BLOCK), jnp.float32, 0.3, 0.7)
    fresh = jnp.clip(jax.random.normal(jax.random.fold_in(key, 2), (NODES, BLOCK), jnp.float32), -5.0, 5.0)
    return (mixing[0][None, :] * basis[:, :BLOCK] - mixing[1][None, :] * basis[:, BLOCK:2 * BLOCK] + fresh).astype(jnp.bfloat16)


def with_ends(result, rng, smallest, largest):
    extent = result.shape
    spot = [jax.random.randint(jax.random.fold_in(rng, axis), (), 0, extent[axis]) for axis in range(len(extent))]
    result = result.at[tuple(spot)].set(smallest)
    longest = extent.index(max(extent))
    spot[longest] = (spot[longest] + 1) % extent[longest]
    return result.at[tuple(spot)].set(largest)


def steps_of(key, dims, pieces, smallest, largest):
    factor_of, own = 1.0, jax.random.fold_in(key, 6)
    for dim, parts in pieces:
        draws = jnp.exp(jax.random.uniform(jax.random.fold_in(own, dim), (parts,), jnp.float32, smallest / len(pieces), largest / len(pieces)))
        factor_of = factor_of * jnp.repeat(draws, dims[dim] // parts).reshape([-1 if axis == dim else 1 for axis in range(len(dims))])
    return factor_of


def setup_inputs(seed: int = 0) -> dict:
    splits = jax.random.split(jax.random.key(seed), 8)
    tiles = jnp.clip(0.099609375 * jax.random.uniform(splits[0], (N_ROW, N_COL, TILES_DEV, TILE, TILE), jnp.float32) ** steps_of(splits[0], (N_ROW, N_COL, TILES_DEV, TILE, TILE), ((0, 16), (1, 16)), -0.2, 0.2), 0.0, 0.099609375).astype(jnp.bfloat16)
    tile_rows = with_ends(jax.random.randint(splits[1], (N_ROW, N_COL, TILES_DEV), 0, NODE_DEV * N_COL // TILE), jax.random.fold_in(splits[1], 1), 0, (NODE_DEV * N_COL // TILE) - 1).astype(jnp.int32)
    tile_cols = with_ends(jax.random.randint(splits[2], (N_ROW, N_COL, TILES_DEV), 0, NODE_DEV * N_ROW // TILE), jax.random.fold_in(splits[2], 1), 0, (NODE_DEV * N_ROW // TILE) - 1).astype(jnp.int32)
    node_level = draw_node_level(jax.random.fold_in(splits[7], 71), 0)
    level_scale = jnp.clip(jnp.exp(jax.random.uniform(splits[4], (LEVELS,), jnp.float32, math.log(0.15), math.log(1.5))), 0.15, 1.5)
    stored_basis = draw_stored_basis(jax.random.fold_in(splits[7], 71), 0)
    start_block = draw_start_block(jax.random.fold_in(splits[7], 71), 0)
    return {"tiles": tiles, "tile_rows": tile_rows, "tile_cols": tile_cols, "node_level": node_level, "level_scale": level_scale, "stored_basis": stored_basis, "start_block": start_block}


def solve_gram(gram_matrix, right_side):
    factor = jnp.linalg.cholesky(gram_matrix)
    partway = lax.linalg.triangular_solve(factor, right_side, left_side=True, lower=True)
    return lax.linalg.triangular_solve(factor, partway, left_side=True, lower=True, transpose_a=True)

def normalize(remainder, squares):
    factor = jnp.linalg.cholesky(squares)
    return lax.linalg.triangular_solve(factor, remainder, left_side=False, lower=True, transpose_a=True)

def similarity(vectors, node_scale, tiles, tile_rows, tile_cols):
    grid_rows = tiles.shape[0]
    grid_cols = tiles.shape[1]
    tile_edge = tiles.shape[3]
    columns = vectors.shape[1]
    scaled = (node_scale[:, None] * vectors.astype(jnp.float32)).astype(jnp.bfloat16)
    pieces_grid = scaled.reshape(grid_rows, grid_cols, -1, columns)
    per_position = pieces_grid.shape[2]
    forward_init = jnp.zeros((grid_rows, grid_cols * per_position // tile_edge, tile_edge, columns), jnp.float32)
    backward_init = jnp.zeros((grid_cols, grid_rows * per_position // tile_edge, tile_edge, columns), jnp.float32)

    def visit_position(carry, position):
        forward_sum, backward_sum = carry
        row_index = (position // grid_cols).astype(jnp.int32)
        col_index = (position % grid_cols).astype(jnp.int32)
        local_tiles = lax.dynamic_index_in_dim(lax.dynamic_index_in_dim(tiles, row_index, 0, False), col_index, 0, False).astype(jnp.float32)
        rows_here = lax.dynamic_index_in_dim(lax.dynamic_index_in_dim(tile_rows, row_index, 0, False), col_index, 0, False)
        cols_here = lax.dynamic_index_in_dim(lax.dynamic_index_in_dim(tile_cols, row_index, 0, False), col_index, 0, False)
        column_block = lax.dynamic_index_in_dim(pieces_grid, col_index, 1, False).reshape(-1, tile_edge, columns).astype(jnp.float32)
        row_block = lax.dynamic_index_in_dim(pieces_grid, row_index, 0, False).reshape(-1, tile_edge, columns).astype(jnp.float32)
        forward_terms = jnp.einsum('tij,tjk->tik', local_tiles, column_block[cols_here])
        backward_terms = jnp.einsum('tji,tjk->tik', local_tiles, row_block[rows_here])
        current = lax.dynamic_index_in_dim(forward_sum, row_index, 0, False).at[rows_here].add(forward_terms)
        forward_sum = lax.dynamic_update_index_in_dim(forward_sum, current, row_index, 0)
        current = lax.dynamic_index_in_dim(backward_sum, col_index, 0, False).at[cols_here].add(backward_terms)
        backward_sum = lax.dynamic_update_index_in_dim(backward_sum, current, col_index, 0)
        return ((forward_sum, backward_sum), None)
    positions = jnp.arange(grid_rows * grid_cols, dtype=jnp.int32)
    (forward_sum, backward_sum), _ = lax.scan(visit_position, (forward_init, backward_init), positions)
    forward_nodes = forward_sum.reshape(-1, columns)
    backward_nodes = backward_sum.reshape(grid_cols, grid_rows, per_position, columns).transpose(1, 0, 2, 3).reshape(-1, columns)
    total = scaled.astype(jnp.float32) + forward_nodes + backward_nodes
    return (node_scale[:, None] * total).astype(jnp.bfloat16)

def extend(basis, image):
    gram_matrix = jnp.dot(basis.T.astype(jnp.float32), basis.astype(jnp.float32), preferred_element_type=jnp.float32)
    cross = jnp.dot(basis.T.astype(jnp.float32), image.astype(jnp.float32), preferred_element_type=jnp.float32)
    coefficients = solve_gram(gram_matrix, cross).astype(jnp.bfloat16)
    remainder = image.astype(jnp.float32) - jnp.dot(basis.astype(jnp.float32), coefficients.astype(jnp.float32), preferred_element_type=jnp.float32)
    squares = jnp.dot(remainder.T, remainder, precision=lax.Precision.HIGHEST) / NODES
    return normalize(remainder, squares).astype(jnp.bfloat16)

def reference(tiles, tile_rows, tile_cols, node_level, level_scale, stored_basis, start_block):
    node_scale = jnp.take(level_scale, node_level, axis=0)
    first_basis = jnp.concatenate([stored_basis, start_block], axis=1)
    image = similarity(start_block, node_scale, tiles, tile_rows, tile_cols)
    first_block = extend(first_basis, image)
    second_basis = jnp.concatenate([first_basis, first_block], axis=1)
    image = similarity(first_block, node_scale, tiles, tile_rows, tile_cols)
    second_block = extend(second_basis, image)
    return (first_block, second_block)
```

```python
import jax
import jax.numpy as jnp
from jax import lax
from jax.experimental import pallas as pl
from jax.experimental.pallas import tpu as pltpu
from jax.sharding import PartitionSpec as P

F32 = jnp.float32
BF16 = jnp.bfloat16
EDGE = 128
BLK = 32
STEP_TILES = 16
NT = (((1,), (1,)), ((), ()))
NN = (((1,), (0,)), ((), ()))
TN = (((0,), (0,)), ((), ()))
VMEM = pltpu.VMEM


def dot(a, b, dims=NN):
    return lax.dot_general(a, b, dims, preferred_element_type=F32)


def dot_exact(a, b, dims=NN):
    return lax.dot_general(
        a, b, dims, preferred_element_type=F32, precision=lax.Precision.HIGHEST
    )


def iota(shape, axis):
    return lax.broadcasted_iota(jnp.int32, shape, axis)


def eye(n, dtype):
    return jnp.where(iota((n, n), 0) == iota((n, n), 1), 1.0, 0.0).astype(dtype)


def whole(count):
    return [pl.BlockSpec(memory_space=VMEM)] * count


def call(body, out_shape, args, scratch=(), vmem=24 << 20):
    return pl.pallas_call(
        body,
        out_shape=out_shape,
        in_specs=whole(len(args)),
        out_specs=jax.tree.map(lambda _: pl.BlockSpec(memory_space=VMEM), out_shape),
        scratch_shapes=list(scratch),
        compiler_params=pltpu.CompilerParams(vmem_limit_bytes=vmem),
    )(*args)


def shape(dims, dtype):
    return jax.ShapeDtypeStruct(dims, dtype)


def spread(block, scale, send_ref, own_ref):
    for j in range(block.shape[1] // EDGE):
        lanes = slice(j * EDGE, (j + 1) * EDGE)
        piece = (scale[:, lanes] * block[:, lanes].astype(F32)).astype(BF16)
        own_ref[j] = piece
        for k in range(send_ref.shape[0]):
            send_ref[k, j] = piece


def prep_body(start_ref, stored_ref, level_ref, levels_ref, send_ref, own_ref, scale_ref, basis_ref):
    table = jnp.broadcast_to(levels_ref[...], (EDGE, EDGE)).T
    for j in range(level_ref.shape[1] // EDGE):
        lanes = slice(j * EDGE, (j + 1) * EDGE)
        member = level_ref[:, lanes] == iota((EDGE, EDGE), 0)
        scale_ref[:, lanes] = jnp.sum(jnp.where(member, table, 0.0), axis=0, keepdims=True)
    start = dot(eye(BLK, BF16), start_ref[...], NT).astype(BF16)
    stored = dot(eye(2 * BLK, BF16), stored_ref[...], NT).astype(BF16)
    basis_ref[0 : 2 * BLK] = stored
    basis_ref[2 * BLK :] = start
    spread(start, scale_ref[...], send_ref, own_ref)


def tile_body(rows_ref, cols_ref, tiles_ref, col_blk, row_blk, fwd_ref, bwd_ref, fwd_acc, bwd_acc):
    step = pl.program_id(0)

    @pl.when(step == 0)
    def _():
        fwd_acc[...] = jnp.zeros_like(fwd_acc)
        bwd_acc[...] = jnp.zeros_like(bwd_acc)

    for t in range(STEP_TILES):
        r = rows_ref[step * STEP_TILES + t]
        c = cols_ref[step * STEP_TILES + t]
        tile = tiles_ref[t]
        fwd_acc[r] += dot(col_blk[c], tile, NT)
        bwd_acc[c] += dot(row_blk[r], tile)

    @pl.when(step == pl.num_programs(0) - 1)
    def _():
        fwd_ref[...] = fwd_acc[...].astype(BF16)
        bwd_ref[...] = bwd_acc[...].astype(BF16)


def tile_pass(rows, cols, tiles, col_blk, row_blk):
    count = tiles.shape[0]
    acc = (row_blk.shape[0], BLK, EDGE)
    blk = pl.BlockSpec(acc, lambda i, *_: (0, 0, 0))
    return pl.pallas_call(
        tile_body,
        out_shape=(shape(acc, BF16), shape(acc, BF16)),
        grid_spec=pltpu.PrefetchScalarGridSpec(
            num_scalar_prefetch=2,
            grid=(count // STEP_TILES,),
            in_specs=[
                pl.BlockSpec((STEP_TILES, EDGE, EDGE), lambda i, *_: (i, 0, 0)),
                blk,
                blk,
            ],
            out_specs=(blk, blk),
            scratch_shapes=[pltpu.VMEM(acc, F32), pltpu.VMEM(acc, F32)],
        ),
        compiler_params=pltpu.CompilerParams(vmem_limit_bytes=24 << 20),
    )(rows, cols, tiles, col_blk, row_blk)


def image_of(fwd_ref, bwd_ref, own_ref, scale_ref):
    pieces = []
    for j in range(own_ref.shape[0]):
        total = own_ref[j].astype(F32)
        for k in range(fwd_ref.shape[0]):
            total += fwd_ref[k, j].astype(F32) + bwd_ref[k, j].astype(F32)
        pieces.append((scale_ref[:, j * EDGE : (j + 1) * EDGE] * total).astype(BF16))
    return jnp.concatenate(pieces, axis=1)


def first_image_body(fwd_ref, bwd_ref, own_ref, scale_ref, basis_ref, all_ref, pay_ref):
    image = image_of(fwd_ref, bwd_ref, own_ref, scale_ref)
    basis = basis_ref[...]
    every = jnp.concatenate([image, basis], axis=0)
    all_ref[...] = every
    stored = basis[0 : 2 * BLK]
    mine = dot(stored, stored, NT)
    pay = jnp.concatenate(
        [
            dot(image, every, NT),
            dot(basis[2 * BLK :], every, NT),
            jnp.concatenate([mine[:BLK], mine[BLK:]], axis=1),
        ],
        axis=0,
    )
    for k in range(pay_ref.shape[0]):
        pay_ref[k] = pay


def second_image_body(fwd_ref, bwd_ref, own_ref, scale_ref, basis_ref, image_ref, pay_ref):
    image = image_of(fwd_ref, bwd_ref, own_ref, scale_ref)
    image_ref[...] = image
    basis = basis_ref[...]
    square = dot(image, image, NT)
    pay = jnp.concatenate(
        [
            dot(image, basis, NT),
            dot(basis[:BLK], basis, NT),
            jnp.concatenate([square, jnp.zeros((BLK, EDGE - BLK), F32)], axis=1),
        ],
        axis=0,
    )
    for k in range(pay_ref.shape[0]):
        pay_ref[k] = pay


def middle_body(got_ref, pay_ref):
    total = jnp.sum(got_ref[...], axis=0)
    for k in range(pay_ref.shape[0]):
        pay_ref[k] = total


def reduce_all(pay):
    got = lax.all_to_all(pay, "row", 0, 0)
    again = call(middle_body, shape(got.shape, F32), (got,))
    return lax.all_to_all(again, "col", 0, 0)


def eliminate(ref, count, first_lane, above):
    rows, width = ref.shape

    def body(k, carry):
        matrix = ref[...]
        row = ref[pl.ds(k, 1), :]
        here = iota((rows, EDGE), 1) == first_lane + k
        column = jnp.sum(jnp.where(here, matrix[:, :EDGE], 0.0), axis=1, keepdims=True)
        pivot = jnp.sum(jnp.where(here[:1], row[:, :EDGE], 0.0), axis=1, keepdims=True)
        index = iota((rows, 1), 0)
        if above:
            scaled = row / pivot
            ref[...] = jnp.where(index == k, scaled, matrix - column * scaled)
        else:
            scaled = row / jnp.sqrt(pivot)
            later = jnp.where(index > k, column / jnp.sqrt(pivot), 0.0)
            ref[...] = jnp.where(index == k, scaled, matrix - later * scaled)
        return carry

    lax.fori_loop(0, count, body, 0)


def pad_lanes(a, width=EDGE):
    return jnp.concatenate([a, jnp.zeros((a.shape[0], width - a.shape[1]), F32)], axis=1)


def inverse_factor(small, square):
    small[...] = pad_lanes(jnp.concatenate([square, eye(BLK, F32)], axis=1))
    eliminate(small, BLK, 0, False)
    return small[:, BLK : 2 * BLK]


def emit(new, out_ref):
    out_ref[...] = dot(new, eye(BLK, BF16), TN).astype(BF16)


def first_solve_body(
    nodes, got_ref, all_ref, scale_ref, first_ref, send_ref, own_ref, next_ref, gram_ref, inv_ref, work, small
):
    got = jnp.sum(got_ref[...], axis=0)
    mine = got[2 * BLK :]
    low = jnp.concatenate(
        [got[:BLK], pltpu.roll(mine, BLK, 1), pltpu.roll(mine, EDGE - BLK, 1), got[BLK : 2 * BLK]], axis=0
    )
    row, lane = iota((EDGE, EDGE), 0), iota((EDGE, EDGE), 1)
    inner_row = (row >= BLK) & (row < 3 * BLK)
    inner_lane = (lane >= BLK) & (lane < 3 * BLK)
    gram = jnp.where(inner_row & jnp.logical_not(inner_lane), low.T, low)
    gram_ref[...] = gram
    work[:, :EDGE] = gram[BLK:]
    work[:, EDGE:] = jnp.where(iota((3 * BLK, EDGE), 0) + BLK == iota((3 * BLK, EDGE), 1), 1.0, 0.0)
    eliminate(work, 3 * BLK, BLK, True)
    inv_ref[...] = jnp.concatenate([jnp.zeros((BLK, EDGE), F32), work[:, EDGE:]], axis=0)
    tall = jnp.concatenate(
        [jnp.where(row[:BLK] == lane[:BLK], 1.0, 0.0), -work[:, :EDGE]], axis=0
    )
    mix = tall.T[:BLK].astype(BF16)
    wide = mix.astype(F32)
    squares = dot_exact(dot_exact(wide, gram), wide, NT) / nodes
    factor = inverse_factor(small, squares)
    remainder = dot(mix, all_ref[...])
    new = dot_exact(factor, remainder).astype(BF16)
    emit(new, first_ref)
    next_ref[...] = jnp.concatenate([new, all_ref[BLK:]], axis=0)
    spread(new, scale_ref[...], send_ref, own_ref)


def second_solve_body(nodes, got_ref, image_ref, basis_ref, gram_ref, inv_ref, second_ref, small):
    got = jnp.sum(got_ref[...], axis=0)
    cross, fresh, square = got[:BLK], got[BLK : 2 * BLK], got[2 * BLK :, :BLK]
    row, lane = iota((EDGE, EDGE), 0), iota((EDGE, EDGE), 1)
    inv = inv_ref[...]
    reach = dot_exact(fresh, inv)
    schur = fresh[:, :BLK] - dot_exact(reach, fresh, NT)
    small[...] = pad_lanes(jnp.concatenate([schur, eye(BLK, F32)], axis=1))
    eliminate(small, BLK, 0, True)
    newest = dot_exact(cross[:, :BLK] - dot_exact(cross, reach, NT), small[:, BLK : 2 * BLK])
    older = dot_exact(cross, inv) - dot_exact(newest, reach)
    coef = jnp.where(lane[:BLK] < BLK, pad_lanes(newest), older).astype(BF16)
    wide = coef.astype(F32)
    full = jnp.concatenate([fresh, jnp.zeros((3 * BLK, EDGE), F32)], axis=0)
    gram = jnp.where(row < BLK, full, jnp.where(lane < BLK, full.T, gram_ref[...]))
    mixed = dot_exact(wide, cross, NT)
    squares = (square - mixed - mixed.T + dot_exact(dot_exact(wide, gram), wide, NT)) / nodes
    factor = inverse_factor(small, squares)
    remainder = image_ref[...].astype(F32) - dot(coef, basis_ref[...])
    emit(dot_exact(factor, remainder).astype(BF16), second_ref)


def per_device(tiles, tile_rows, tile_cols, node_level, level_scale, stored_basis, start_block):
    tile_stack = tiles.reshape(tiles.shape[2:])
    rows, cols = tile_rows.reshape(-1), tile_cols.reshape(-1)
    side = lax.axis_size("row")
    held = stored_basis.shape[0]
    nodes = held * side * lax.axis_size("col")
    pieces = held // EDGE
    send_shape = shape((side, pieces, BLK, EDGE), BF16)
    own_shape = shape((pieces, BLK, EDGE), BF16)

    def product(send):
        col_blk = lax.all_to_all(send, "row", 0, 0).reshape(-1, BLK, EDGE)
        row_blk = lax.all_to_all(send, "col", 0, 0).reshape(-1, BLK, EDGE)
        fwd, bwd = tile_pass(rows, cols, tile_stack, col_blk, row_blk)
        fwd = lax.all_to_all(fwd.reshape(send.shape), "col", 0, 0)
        bwd = lax.all_to_all(bwd.reshape(send.shape), "row", 0, 0)
        return fwd, bwd

    send, own, scale, basis = call(
        prep_body,
        (send_shape, own_shape, shape((1, held), F32), shape((3 * BLK, held), BF16)),
        (start_block, stored_basis, node_level.reshape(1, -1), level_scale.reshape(1, -1)),
    )
    fwd, bwd = product(send)
    pay_shape = shape((side, 3 * BLK, EDGE), F32)
    every, pay = call(
        first_image_body, (shape((EDGE, held), BF16), pay_shape), (fwd, bwd, own, scale, basis)
    )
    got = reduce_all(pay)
    square_shape = shape((EDGE, EDGE), F32)
    first, send, own, basis, gram, inv = call(
        lambda *refs: first_solve_body(nodes, *refs),
        (
            shape((held, BLK), BF16),
            send_shape,
            own_shape,
            shape((EDGE, held), BF16),
            square_shape,
            square_shape,
        ),
        (got, every, scale),
        (pltpu.VMEM((3 * BLK, 2 * EDGE), F32), pltpu.VMEM((BLK, EDGE), F32)),
    )
    fwd, bwd = product(send)
    image, pay = call(
        second_image_body, (shape((BLK, held), BF16), pay_shape), (fwd, bwd, own, scale, basis)
    )
    got = reduce_all(pay)
    second = call(
        lambda *refs: second_solve_body(nodes, *refs),
        shape((held, BLK), BF16),
        (got, image, basis, gram, inv),
        (pltpu.VMEM((BLK, EDGE), F32),),
    )
    return (first, second)


def solution(mesh):
    return jax.shard_map(
        per_device,
        mesh=mesh,
        in_specs=(
            P("row", "col", None, None, None),
            P("row", "col", None),
            P("row", "col", None),
            P(("row", "col")),
            P(),
            P(("row", "col"), None),
            P(("row", "col"), None),
        ),
        out_specs=(P(("row", "col"), None), P(("row", "col"), None)),
        check_vma=False,
    )
```

```python
import jax
import jax.numpy as jnp
from jax import lax
from jax.experimental import pallas as pl
from jax.experimental.pallas import tpu as pltpu
from jax.sharding import PartitionSpec as P

F32 = jnp.float32
BF16 = jnp.bfloat16
EDGE = 128
BLK = 32
CHUNK = 80
NT = (((1,), (1,)), ((), ()))
NN = (((1,), (0,)), ((), ()))
VMEM = pltpu.VMEM


def dot(a, b, dims=NN):
    return lax.dot_general(a, b, dims, preferred_element_type=F32)


def dot_exact(a, b, dims=NN):
    return lax.dot_general(
        a, b, dims, preferred_element_type=F32, precision=lax.Precision.HIGHEST
    )


def iota(shape, axis):
    return lax.broadcasted_iota(jnp.int32, shape, axis)


def eye(n, dtype):
    return jnp.where(iota((n, n), 0) == iota((n, n), 1), 1.0, 0.0).astype(dtype)


def whole(count):
    return [pl.BlockSpec(memory_space=VMEM)] * count


def call(body, out_shape, args, scratch=(), vmem=24 << 20):
    return pl.pallas_call(
        body,
        out_shape=out_shape,
        in_specs=whole(len(args)),
        out_specs=jax.tree.map(lambda _: pl.BlockSpec(memory_space=VMEM), out_shape),
        scratch_shapes=list(scratch),
        compiler_params=pltpu.CompilerParams(vmem_limit_bytes=vmem),
    )(*args)


def shape(dims, dtype):
    return jax.ShapeDtypeStruct(dims, dtype)


def spread(block, scale, send_ref, own_ref):
    for j in range(block.shape[1] // EDGE):
        lanes = slice(j * EDGE, (j + 1) * EDGE)
        piece = (scale[:, lanes] * block[:, lanes].astype(F32)).astype(BF16)
        own_ref[j] = piece
        for k in range(send_ref.shape[0]):
            send_ref[k, j] = piece


def prep_body(start_in, stored_in, level_in, levels_in, send_ref, own_ref, scale_ref, basis_ref, level_ref, levels_ref, done):
    copies = [
        pltpu.make_async_copy(src, dst, done.at[i])
        for i, (src, dst) in enumerate(
            (
                (level_in, level_ref),
                (levels_in, levels_ref),
                (start_in, basis_ref.at[2 * BLK : 3 * BLK]),
                (stored_in, basis_ref.at[0 : 2 * BLK]),
            )
        )
    ]
    for copy in copies:
        copy.start()
    for copy in copies:
        copy.wait()
    table = jnp.broadcast_to(levels_ref[...], (EDGE, EDGE)).T
    for j in range(level_ref.shape[1] // EDGE):
        lanes = slice(j * EDGE, (j + 1) * EDGE)
        member = level_ref[:, lanes] == iota((EDGE, EDGE), 0)
        scale_ref[:, lanes] = jnp.sum(jnp.where(member, table, 0.0), axis=0, keepdims=True)
    spread(basis_ref[2 * BLK :], scale_ref[...], send_ref, own_ref)


def prep(send_shape, own_shape, start, stored, level, levels):
    held = start.shape[1]
    outs = (send_shape, own_shape, shape((1, held), F32), shape((3 * BLK, held), BF16))
    return pl.pallas_call(
        prep_body,
        out_shape=outs,
        in_specs=[pl.BlockSpec(memory_space=pltpu.HBM)] * 4,
        out_specs=tuple(whole(4)),
        scratch_shapes=[
            pltpu.VMEM(level.shape, jnp.int32),
            pltpu.VMEM(levels.shape, F32),
            pltpu.SemaphoreType.DMA((4,)),
        ],
        compiler_params=pltpu.CompilerParams(vmem_limit_bytes=58 << 20),
    )(start, stored, level, levels)


def pair_rows(first, second):
    none = jnp.zeros_like(first)
    return jnp.concatenate(
        [jnp.concatenate([first, none], axis=1), jnp.concatenate([none, second], axis=1)], axis=0
    )


def tile_body(
    pieces, me_ref, rows_ref, cols_ref, tiles_ref, col_in, near_in, far_in, bwd_out, keep_out, away_out,
    col_blk, row_blk, fwd_acc, bwd_acc, bwd_ref, keep_ref, away_ref, held, done, moved,
):
    chunks = held.shape[0]
    half = near_in.shape[0]

    def copy(i):
        part = tiles_ref.at[pl.ds(i * CHUNK, CHUNK)]
        return pltpu.make_async_copy(part, held.at[i], done.at[i])

    ins = [
        pltpu.make_async_copy(src, dst, moved.at[i])
        for i, (src, dst) in enumerate(
            ((col_in, col_blk), (near_in, row_blk.at[0:half]), (far_in, row_blk.at[half : 2 * half]))
        )
    ]
    outs = [
        pltpu.make_async_copy(src, dst, moved.at[3 + i])
        for i, (src, dst) in enumerate(((bwd_ref, bwd_out), (keep_ref, keep_out), (away_ref, away_out)))
    ]
    copy(0).start()
    for move in ins:
        move.start()
    for i in range(1, chunks):
        copy(i).start()
    fwd_acc[...] = jnp.zeros_like(fwd_acc)
    bwd_acc[...] = jnp.zeros_like(bwd_acc)
    me = me_ref[0]

    def place(row):
        apart = (row // pieces) ^ me
        return ((apart & 1) * 8 + (apart >> 1)) * pieces + (row & (pieces - 1))

    def body(i, carry):
        copy(i).wait()
        for t in range(0, CHUNK, 2):
            r = [place(rows_ref[0, 0, i * CHUNK + t + n]) for n in range(2)]
            c = [cols_ref[0, 0, i * CHUNK + t + n] for n in range(2)]
            one, two = held[i, t], held[i, t + 1]
            terms = dot(pair_rows(col_blk[c[0]], col_blk[c[1]]), jnp.concatenate([one, two], axis=1), NT)
            fwd_acc[r[0]] += terms[:BLK]
            fwd_acc[r[1]] += terms[BLK:]
            terms = dot(pair_rows(row_blk[r[0]], row_blk[r[1]]), jnp.concatenate([one, two], axis=0))
            bwd_acc[c[0]] += terms[:BLK]
            bwd_acc[c[1]] += terms[BLK:]
        return carry

    for move in ins:
        move.wait()
    lax.fori_loop(0, chunks, body, 0)
    bwd_ref[...] = bwd_acc[...].astype(BF16)
    outs[0].start()
    away_ref[...] = fwd_acc[half:].astype(BF16)
    outs[2].start()
    keep_ref[...] = fwd_acc[:half].astype(BF16)
    outs[1].start()
    for move in outs:
        move.wait()


def tile_pass(pieces, me, rows, cols, tiles, col_blk, near, far):
    count = tiles.shape[0]
    half = near.shape
    acc = col_blk.shape
    scalars = pl.BlockSpec(memory_space=pltpu.SMEM)
    return pl.pallas_call(
        lambda *refs: tile_body(pieces, *refs),
        out_shape=(shape(acc, BF16), shape(half, BF16), shape(half, BF16)),
        in_specs=[scalars] * 3 + [pl.BlockSpec(memory_space=pltpu.HBM)] + [pl.BlockSpec(memory_space=pl.ANY)] * 3,
        out_specs=tuple([pl.BlockSpec(memory_space=pl.ANY)] * 3),
        scratch_shapes=[
            pltpu.VMEM(acc, BF16),
            pltpu.VMEM(acc, BF16),
            pltpu.VMEM(acc, F32),
            pltpu.VMEM(acc, F32),
            pltpu.VMEM(acc, BF16),
            pltpu.VMEM(half, BF16),
            pltpu.VMEM(half, BF16),
            pltpu.VMEM((count // CHUNK, CHUNK, EDGE, EDGE), BF16),
            pltpu.SemaphoreType.DMA((count // CHUNK,)),
            pltpu.SemaphoreType.DMA((6,)),
        ],
        cost_estimate=pl.CostEstimate(flops=8_000_000_000, bytes_accessed=14_000_000, transcendentals=0),
        compiler_params=pltpu.CompilerParams(vmem_limit_bytes=51 << 20),
    )(me, rows, cols, tiles, col_blk, near, far)


def keep_body(in_ref, out_ref):
    pass


def arrive(a):
    return pl.pallas_call(
        keep_body,
        out_shape=shape(a.shape, a.dtype),
        in_specs=[pl.BlockSpec(memory_space=pl.ANY)],
        out_specs=pl.BlockSpec(memory_space=pl.ANY),
        input_output_aliases={0: 0},
        cost_estimate=pl.CostEstimate(flops=40_000_000_000, bytes_accessed=1_000_000, transcendentals=0),
        compiler_params=pltpu.CompilerParams(vmem_limit_bytes=1 << 20),
    )(a)


def swap(a, mask):
    return lax.ppermute(a, "col", [(i, i ^ mask) for i in range(lax.axis_size("col"))])


def gather_col(own):
    two = jnp.concatenate([own, swap(own, 2)], axis=0)
    eight = jnp.concatenate([two] + [swap(two, 4 * j) for j in range(1, 4)], axis=0)
    return (eight, swap(eight, 1))


def halve_body(parts, *refs):
    ins, outs = refs[: -1 - parts], refs[-1 - parts :]
    total = ins[0][...].astype(F32)
    for ref in ins[1:]:
        total = total + ref[...].astype(F32)
    size = total.shape[0] // (1 + parts)
    for i, ref in enumerate(outs):
        ref[...] = total[i * size : (i + 1) * size].astype(ref.dtype)


def halve(parts, keep, *arrived):
    piece = (keep.shape[0] // (1 + parts),) + keep.shape[1:]
    outs = (shape(piece, F32),) + (shape(piece, BF16),) * parts
    return call(lambda *refs: halve_body(parts, *refs), outs, (keep, *arrived))


def scatter_col(keep, send):
    keep, *sends = halve(3, keep, swap(send, 1))
    arrived = [swap(send, 4 * (j + 1)) for j, send in enumerate(sends)]
    keep, send = halve(1, keep, *arrived)
    return keep, swap(send, 2)


def image_of(keep_ref, fwd_ref, bwd_ref, own_ref, scale_ref):
    pieces = []
    for j in range(own_ref.shape[0]):
        total = own_ref[j].astype(F32) + keep_ref[j] + fwd_ref[j].astype(F32)
        for k in range(bwd_ref.shape[0]):
            total += bwd_ref[k, j].astype(F32)
        pieces.append((scale_ref[:, j * EDGE : (j + 1) * EDGE] * total).astype(BF16))
    return jnp.concatenate(pieces, axis=1)


def share(core_ref, halves, keep_ref, send_ref):
    mine = (core_ref[0] & 1) == 0
    keep_ref[...] = jnp.where(mine, halves[0], halves[1])
    send_ref[...] = jnp.where(mine, halves[1], halves[0])


def first_image_body(core_ref, keep_ref, fwd_ref, bwd_ref, own_ref, scale_ref, basis_ref, all_ref, mine_ref, send_ref):
    image = image_of(keep_ref, fwd_ref, bwd_ref, own_ref, scale_ref)
    basis = basis_ref[...]
    every = jnp.concatenate([image, basis], axis=0)
    all_ref[...] = every
    stored = basis[0 : 2 * BLK]
    inner = dot(stored, stored, NT)
    inner = jnp.concatenate([inner[:BLK], inner[BLK:]], axis=1)
    halves = [
        jnp.concatenate([dot(image, every, NT), inner[: BLK // 2]], axis=0),
        jnp.concatenate([dot(basis[2 * BLK :], every, NT), inner[BLK // 2 :]], axis=0),
    ]
    share(core_ref, halves, mine_ref, send_ref)


def second_image_body(core_ref, keep_ref, fwd_ref, bwd_ref, own_ref, scale_ref, basis_ref, image_ref, mine_ref, send_ref):
    image = image_of(keep_ref, fwd_ref, bwd_ref, own_ref, scale_ref)
    image_ref[...] = image
    basis = basis_ref[...]
    square = dot(image, image, NT)
    square = jnp.concatenate([square[8 * i : 8 * i + 8] for i in range(4)], axis=1)
    halves = [
        jnp.concatenate([dot(image, basis, NT), square], axis=0),
        jnp.concatenate([dot(basis[:BLK], basis, NT), jnp.zeros((8, EDGE), F32)], axis=0),
    ]
    share(core_ref, halves, mine_ref, send_ref)


def image_call(body, out, rows, core, args):
    half = shape((rows, EDGE), F32)
    return pl.pallas_call(
        body,
        out_shape=(out, half, half),
        in_specs=[pl.BlockSpec(memory_space=pltpu.SMEM)] + whole(len(args)),
        out_specs=tuple(whole(3)),
        compiler_params=pltpu.CompilerParams(vmem_limit_bytes=24 << 20),
    )(core, *args)


def repeat_body(*refs):
    total = refs[0][...]
    for ref in refs[1:-1]:
        total = total + ref[...]
    total = total.reshape((-1,) + refs[-1].shape[1:]).sum(axis=0)
    for k in range(refs[-1].shape[0]):
        refs[-1][k] = total


def reduce_all(keep, send):
    side = lax.axis_size("row")
    out = shape((side,) + keep.shape, F32)
    got = lax.all_to_all(call(repeat_body, out, (keep, swap(send, 1))), "row", 0, 0)
    return lax.all_to_all(call(repeat_body, out, (got,)), "col", 0, 0)


def sum_halves(got_ref):
    halves = []
    for core in range(2):
        total = got_ref[core]
        for k in range(core + 2, got_ref.shape[0], 2):
            total = total + got_ref[k]
        halves.append(total)
    return halves


def eliminate(tiles, count, first):
    shape_of = tiles[0].shape
    index = iota(shape_of, 0)
    for base in range(0, count, 4):
        columns = [
            jnp.broadcast_to(tiles[0][:, first + base + a : first + base + a + 1], shape_of) for a in range(4)
        ]
        rows = [[tile[base + a : base + a + 1] for tile in tiles] for a in range(4)]
        factors = []
        done = []
        for a in range(4):
            pivot = columns[a][base + a : base + a + 1]
            inverse = 1.0 / pivot
            for c in range(a + 1, 4):
                lower = columns[a][base + c : base + c + 1] * inverse
                upper = columns[c][base + a : base + a + 1] * inverse
                rows[c] = [row - lower * top for row, top in zip(rows[c], rows[a])]
                columns[c] = columns[c] - columns[a] * upper
            factors.append(jnp.where(index >= base + 4, columns[a] * inverse, 0.0))
            root = jnp.sqrt(pivot)
            done.append([row / root for row in rows[a]])
        tiles = list(tiles)
        for i in range(len(tiles)):
            tile = tiles[i]
            for a in range(4):
                tile = tile - factors[a] * rows[a][i]
            for a in range(4):
                tile = jnp.where(index == base + a, done[a][i], tile)
            tiles[i] = tile
    return tiles


def pad_lanes(a, width=EDGE):
    return jnp.concatenate([a, jnp.zeros((a.shape[0], width - a.shape[1]), F32)], axis=1)


def inverse_factor(square):
    both = pad_lanes(jnp.concatenate([square, eye(BLK, F32)], axis=1))
    return eliminate([both], BLK, 0)[0][:, BLK : 2 * BLK]


def first_solve_body(
    nodes, got_ref, all_ref, scale_ref, first_ref, send_ref, own_ref, next_ref, gram_ref, inv_ref
):
    top, bottom = sum_halves(got_ref)
    mine = jnp.concatenate([top[BLK:], bottom[BLK:]], axis=0)
    low = jnp.concatenate(
        [top[:BLK], pltpu.roll(mine, BLK, 1), pltpu.roll(mine, EDGE - BLK, 1), bottom[:BLK]], axis=0
    )
    row, lane = iota((EDGE, EDGE), 0), iota((EDGE, EDGE), 1)
    inner_row = (row >= BLK) & (row < 3 * BLK)
    inner_lane = (lane >= BLK) & (lane < 3 * BLK)
    gram = jnp.where(inner_row & jnp.logical_not(inner_lane), low.T, low)
    gram_ref[...] = gram
    unit = jnp.where(row[BLK:] == lane[BLK:], 1.0, 0.0)
    lower = eliminate([gram[BLK:], unit], 3 * BLK, BLK)[1]
    lower = jnp.concatenate([jnp.zeros((BLK, EDGE), F32), lower], axis=0)
    inv = dot_exact(lower.T, lower)
    inv_ref[...] = inv
    coef = dot_exact(gram[:BLK], inv)
    mix = jnp.where(lane[:BLK] < BLK, jnp.where(row[:BLK] == lane[:BLK], 1.0, 0.0), -coef).astype(BF16)
    wide = mix.astype(F32)
    squares = dot_exact(dot_exact(wide, gram), wide, NT) / nodes
    factor = inverse_factor(squares)
    remainder = dot(mix, all_ref[...])
    new = dot_exact(factor, remainder).astype(BF16)
    first_ref[...] = new
    next_ref[...] = jnp.concatenate([new, all_ref[BLK:]], axis=0)
    spread(new, scale_ref[...], send_ref, own_ref)


def second_solve_body(nodes, got_ref, image_ref, basis_ref, gram_ref, inv_ref, second_ref):
    top, bottom = sum_halves(got_ref)
    cross, fresh = top[:BLK], bottom[:BLK]
    square = jnp.concatenate([top[BLK:, BLK * i : BLK * (i + 1)] for i in range(4)], axis=0)
    row, lane = iota((EDGE, EDGE), 0), iota((EDGE, EDGE), 1)
    inv = inv_ref[...]
    reach = dot_exact(fresh, inv)
    schur = fresh[:, :BLK] - dot_exact(reach, fresh, NT)
    lower = inverse_factor(schur)
    newest = dot_exact(dot_exact(cross[:, :BLK] - dot_exact(cross, reach, NT), lower, NT), lower)
    older = dot_exact(cross, inv) - dot_exact(newest, reach)
    coef = jnp.where(lane[:BLK] < BLK, pad_lanes(newest), older).astype(BF16)
    wide = coef.astype(F32)
    full = jnp.concatenate([fresh, jnp.zeros((3 * BLK, EDGE), F32)], axis=0)
    gram = jnp.where(row < BLK, full, jnp.where(lane < BLK, full.T, gram_ref[...]))
    mixed = dot_exact(wide, cross, NT)
    squares = (square - mixed - mixed.T + dot_exact(dot_exact(wide, gram), wide, NT)) / nodes
    factor = inverse_factor(squares)
    remainder = image_ref[...].astype(F32) - dot(coef, basis_ref[...])
    second_ref[...] = dot_exact(factor, remainder).astype(BF16)


def per_device(tiles, tile_rows, tile_cols, node_level, level_scale, stored_basis, start_block):
    tile_stack = tiles.reshape(tiles.shape[2:])
    side = lax.axis_size("row")
    held = stored_basis.shape[0]
    nodes = held * side * lax.axis_size("col")
    pieces = held // EDGE
    me = lax.axis_index("col").reshape(1)
    send_shape = shape((side, pieces, BLK, EDGE), BF16)
    own_shape = shape((pieces, BLK, EDGE), BF16)

    def product(send, own):
        col_blk = arrive(lax.all_to_all(send, "row", 0, 0).reshape(-1, BLK, EDGE))
        near, far = gather_col(own)
        bwd, keep, away = tile_pass(pieces, me, tile_rows, tile_cols, tile_stack, col_blk, near, far)
        bwd = lax.all_to_all(bwd.reshape(send.shape), "row", 0, 0)
        keep, fwd = scatter_col(keep, away)
        return keep, fwd, bwd

    send, own, scale, basis = prep(
        send_shape,
        own_shape,
        start_block.T,
        stored_basis.T,
        node_level.reshape(1, -1),
        level_scale.reshape(1, -1),
    )
    parts = product(send, own)
    every, keep, away = image_call(
        first_image_body, shape((EDGE, held), BF16), 3 * BLK // 2, me, (*parts, own, scale, basis)
    )
    got = reduce_all(keep, away)
    square_shape = shape((EDGE, EDGE), F32)
    first, send, own, basis, gram, inv = call(
        lambda *refs: first_solve_body(nodes, *refs),
        (
            shape((BLK, held), BF16),
            send_shape,
            own_shape,
            shape((EDGE, held), BF16),
            square_shape,
            square_shape,
        ),
        (got, every, scale),
    )
    parts = product(send, own)
    image, keep, away = image_call(
        second_image_body, shape((BLK, held), BF16), BLK + 8, me, (*parts, own, scale, basis)
    )
    got = reduce_all(keep, away)
    second = call(
        lambda *refs: second_solve_body(nodes, *refs),
        shape((BLK, held), BF16),
        (got, image, basis, gram, inv),
    )
    return (first.T, second.T)


def solution(mesh):
    return jax.shard_map(
        per_device,
        mesh=mesh,
        in_specs=(
            P("row", "col", None, None, None),
            P("row", "col", None),
            P("row", "col", None),
            P(("row", "col")),
            P(),
            P(("row", "col"), None),
            P(("row", "col"), None),
        ),
        out_specs=(P(("row", "col"), None), P(("row", "col"), None)),
        check_vma=False,
    )
```

```python
import jax
import jax.numpy as jnp
from jax import lax
from jax.experimental import pallas as pl
from jax.experimental.pallas import tpu as pltpu
from jax.sharding import PartitionSpec as P

F32 = jnp.float32
BF16 = jnp.bfloat16
EDGE = 128
BLK = 32
CHUNK = 80
WIDE = 8
NT = (((1,), (1,)), ((), ()))
NN = (((1,), (0,)), ((), ()))
VMEM = pltpu.VMEM


def dot(a, b, dims=NN):
    return lax.dot_general(a, b, dims, preferred_element_type=F32)


def dot_exact(a, b, dims=NN):
    return lax.dot_general(
        a, b, dims, preferred_element_type=F32, precision=lax.Precision.HIGHEST
    )


def iota(shape, axis):
    return lax.broadcasted_iota(jnp.int32, shape, axis)


def eye(n, dtype):
    return jnp.where(iota((n, n), 0) == iota((n, n), 1), 1.0, 0.0).astype(dtype)


def whole(count):
    return [pl.BlockSpec(memory_space=VMEM)] * count


def call(body, out_shape, args, scratch=(), vmem=24 << 20):
    return pl.pallas_call(
        body,
        out_shape=out_shape,
        in_specs=whole(len(args)),
        out_specs=jax.tree.map(lambda _: pl.BlockSpec(memory_space=VMEM), out_shape),
        scratch_shapes=list(scratch),
        compiler_params=pltpu.CompilerParams(vmem_limit_bytes=vmem),
    )(*args)


def shape(dims, dtype):
    return jax.ShapeDtypeStruct(dims, dtype)


def spread(block, scale, send_ref, own_ref):
    for j in range(block.shape[1] // EDGE):
        lanes = slice(j * EDGE, (j + 1) * EDGE)
        piece = (scale[:, lanes] * block[:, lanes].astype(F32)).astype(BF16)
        own_ref[j] = piece
        for k in range(send_ref.shape[0]):
            send_ref[k, j] = piece


def prep_body(start_in, stored_in, level_in, levels_in, send_ref, own_ref, scale_ref, basis_ref, level_ref, levels_ref, done):
    copies = [
        pltpu.make_async_copy(src, dst, done.at[i])
        for i, (src, dst) in enumerate(
            (
                (level_in, level_ref),
                (levels_in, levels_ref),
                (start_in, basis_ref.at[2 * BLK : 3 * BLK]),
                (stored_in, basis_ref.at[0 : 2 * BLK]),
            )
        )
    ]
    for copy in copies:
        copy.start()
    for copy in copies:
        copy.wait()
    table = jnp.broadcast_to(levels_ref[...], (EDGE, EDGE)).T
    for j in range(level_ref.shape[1] // EDGE):
        lanes = slice(j * EDGE, (j + 1) * EDGE)
        member = level_ref[:, lanes] == iota((EDGE, EDGE), 0)
        scale_ref[:, lanes] = jnp.sum(jnp.where(member, table, 0.0), axis=0, keepdims=True)
    spread(basis_ref[2 * BLK :], scale_ref[...], send_ref, own_ref)


def prep(send_shape, own_shape, start, stored, level, levels):
    held = start.shape[1]
    outs = (send_shape, own_shape, shape((1, held), F32), shape((3 * BLK, held), BF16))
    return pl.pallas_call(
        prep_body,
        out_shape=outs,
        in_specs=[pl.BlockSpec(memory_space=pltpu.HBM)] * 4,
        out_specs=tuple(whole(4)),
        scratch_shapes=[
            pltpu.VMEM(level.shape, jnp.int32),
            pltpu.VMEM(levels.shape, F32),
            pltpu.SemaphoreType.DMA((4,)),
        ],
        compiler_params=pltpu.CompilerParams(vmem_limit_bytes=58 << 20),
    )(start, stored, level, levels)


def pair_rows(first, second):
    none = jnp.zeros_like(first)
    return jnp.concatenate(
        [jnp.concatenate([first, none], axis=1), jnp.concatenate([none, second], axis=1)], axis=0
    )


def tile_body(
    pieces, me_ref, rows_ref, cols_ref, tiles_ref, col_in, near_in, far_in, bwd_out, keep_out, away_out,
    col_blk, row_blk, fwd_acc, bwd_acc, bwd_ref, keep_ref, away_ref, held, done, moved,
):
    chunks = held.shape[0]
    half = near_in.shape[0]

    def copy(i):
        part = tiles_ref.at[pl.ds(i * CHUNK, CHUNK)]
        return pltpu.make_async_copy(part, held.at[i], done.at[i])

    ins = [
        pltpu.make_async_copy(src, dst, moved.at[i])
        for i, (src, dst) in enumerate(
            ((col_in, col_blk), (near_in, row_blk.at[0:half]), (far_in, row_blk.at[half : 2 * half]))
        )
    ]
    outs = [
        pltpu.make_async_copy(src, dst, moved.at[3 + i])
        for i, (src, dst) in enumerate(((bwd_ref, bwd_out), (keep_ref, keep_out), (away_ref, away_out)))
    ]
    copy(0).start()
    for move in ins:
        move.start()
    for i in range(1, chunks):
        copy(i).start()
    fwd_acc[...] = jnp.zeros_like(fwd_acc)
    bwd_acc[...] = jnp.zeros_like(bwd_acc)
    me = me_ref[0]

    def place(row):
        apart = (row // pieces) ^ me
        return ((apart & 1) * 8 + (apart >> 1)) * pieces + (row & (pieces - 1))

    def body(i, carry):
        copy(i).wait()
        for t in range(0, CHUNK, 2):
            r = [place(rows_ref[0, 0, i * CHUNK + t + n]) for n in range(2)]
            c = [cols_ref[0, 0, i * CHUNK + t + n] for n in range(2)]
            one, two = held[i, t], held[i, t + 1]
            terms = dot(pair_rows(col_blk[c[0]], col_blk[c[1]]), jnp.concatenate([one, two], axis=1), NT)
            fwd_acc[r[0]] += terms[:BLK]
            fwd_acc[r[1]] += terms[BLK:]
            terms = dot(pair_rows(row_blk[r[0]], row_blk[r[1]]), jnp.concatenate([one, two], axis=0))
            bwd_acc[c[0]] += terms[:BLK]
            bwd_acc[c[1]] += terms[BLK:]
        return carry

    for move in ins:
        move.wait()
    lax.fori_loop(0, chunks, body, 0)
    bwd_ref[...] = bwd_acc[...].astype(BF16)
    outs[0].start()
    away_ref[...] = fwd_acc[half:].astype(BF16)
    outs[2].start()
    keep_ref[...] = fwd_acc[:half].astype(BF16)
    outs[1].start()
    for move in outs:
        move.wait()


def tile_pass(pieces, me, rows, cols, tiles, col_blk, near, far):
    count = tiles.shape[0]
    half = near.shape
    acc = col_blk.shape
    scalars = pl.BlockSpec(memory_space=pltpu.SMEM)
    return pl.pallas_call(
        lambda *refs: tile_body(pieces, *refs),
        out_shape=(shape(acc, BF16), shape(half, BF16), shape(half, BF16)),
        in_specs=[scalars] * 3 + [pl.BlockSpec(memory_space=pltpu.HBM)] + [pl.BlockSpec(memory_space=pl.ANY)] * 3,
        out_specs=tuple([pl.BlockSpec(memory_space=pl.ANY)] * 3),
        scratch_shapes=[
            pltpu.VMEM(acc, BF16),
            pltpu.VMEM(acc, BF16),
            pltpu.VMEM(acc, F32),
            pltpu.VMEM(acc, F32),
            pltpu.VMEM(acc, BF16),
            pltpu.VMEM(half, BF16),
            pltpu.VMEM(half, BF16),
            pltpu.VMEM((count // CHUNK, CHUNK, EDGE, EDGE), BF16),
            pltpu.SemaphoreType.DMA((count // CHUNK,)),
            pltpu.SemaphoreType.DMA((6,)),
        ],
        cost_estimate=pl.CostEstimate(flops=8_000_000_000, bytes_accessed=14_000_000, transcendentals=0),
        compiler_params=pltpu.CompilerParams(vmem_limit_bytes=51 << 20),
    )(me, rows, cols, tiles, col_blk, near, far)


def keep_body(in_ref, out_ref):
    pass


def arrive(a):
    return pl.pallas_call(
        keep_body,
        out_shape=shape(a.shape, a.dtype),
        in_specs=[pl.BlockSpec(memory_space=pl.ANY)],
        out_specs=pl.BlockSpec(memory_space=pl.ANY),
        input_output_aliases={0: 0},
        cost_estimate=pl.CostEstimate(flops=40_000_000_000, bytes_accessed=1_000_000, transcendentals=0),
        compiler_params=pltpu.CompilerParams(vmem_limit_bytes=1 << 20),
    )(a)


def swap(a, mask):
    return lax.ppermute(a, "col", [(i, i ^ mask) for i in range(lax.axis_size("col"))])


def gather_col(own):
    two = jnp.concatenate([own, swap(own, 2)], axis=0)
    eight = jnp.concatenate([two] + [swap(two, 4 * j) for j in range(1, 4)], axis=0)
    return (eight, swap(eight, 1))


def halve_body(parts, *refs):
    ins, outs = refs[: -1 - parts], refs[-1 - parts :]
    total = ins[0][...].astype(F32)
    for ref in ins[1:]:
        total = total + ref[...].astype(F32)
    size = total.shape[0] // (1 + parts)
    for i, ref in enumerate(outs):
        ref[...] = total[i * size : (i + 1) * size].astype(ref.dtype)


def halve(parts, keep, *arrived):
    piece = (keep.shape[0] // (1 + parts),) + keep.shape[1:]
    outs = (shape(piece, F32),) + (shape(piece, BF16),) * parts
    return call(lambda *refs: halve_body(parts, *refs), outs, (keep, *arrived))


def scatter_col(keep, send):
    keep, *sends = halve(3, keep, swap(send, 1))
    arrived = [swap(send, 4 * (j + 1)) for j, send in enumerate(sends)]
    keep, send = halve(1, keep, *arrived)
    return keep, swap(send, 2)


def image_of(keep_ref, fwd_ref, bwd_ref, own_ref, scale_ref):
    pieces = []
    for j in range(own_ref.shape[0]):
        total = own_ref[j].astype(F32) + keep_ref[j] + fwd_ref[j].astype(F32)
        for k in range(bwd_ref.shape[0]):
            total += bwd_ref[k, j].astype(F32)
        pieces.append((scale_ref[:, j * EDGE : (j + 1) * EDGE] * total).astype(BF16))
    return jnp.concatenate(pieces, axis=1)


def first_image_body(keep_ref, fwd_ref, bwd_ref, own_ref, scale_ref, basis_ref, all_ref, pay_ref):
    image = image_of(keep_ref, fwd_ref, bwd_ref, own_ref, scale_ref)
    basis = basis_ref[...]
    every = jnp.concatenate([image, basis], axis=0)
    all_ref[...] = every
    stored = basis[0 : 2 * BLK]
    inner = dot(stored, stored, NT)
    inner = jnp.concatenate([inner[:BLK], inner[BLK:]], axis=1)
    pay_ref[0:BLK] = dot(image, every, NT)
    pay_ref[BLK : 2 * BLK] = dot(basis[2 * BLK :], every, NT)
    pay_ref[2 * BLK :] = inner


def second_image_body(keep_ref, fwd_ref, bwd_ref, own_ref, scale_ref, basis_ref, image_ref, pay_ref):
    image = image_of(keep_ref, fwd_ref, bwd_ref, own_ref, scale_ref)
    image_ref[...] = image
    basis = basis_ref[...]
    square = dot(image, image, NT)
    pay_ref[0:BLK] = dot(image, basis, NT)
    pay_ref[BLK : 2 * BLK] = dot(basis[:BLK], basis, NT)
    pay_ref[2 * BLK :] = jnp.concatenate([square[8 * i : 8 * i + 8] for i in range(4)], axis=1)


def sum_body(*refs):
    total = refs[0][...]
    for ref in refs[1:-1]:
        total = total + ref[...]
    refs[-1][...] = total


def swap_row(a, mask):
    return lax.ppermute(a, "row", [(i, i ^ mask) for i in range(lax.axis_size("row"))])


def reduce_all(pay):
    for exchange, masks in ORDER:
        others = [exchange(pay, mask) for mask in masks]
        pay = call(sum_body, shape(pay.shape, F32), (pay, *others))
    return pay


ORDER = ((swap, (1,)), (swap_row, (1, 2, 3)), (swap_row, (4, 8, 12)), (swap, (4, 8, 12)), (swap, (2,)))


def eliminate(tiles, count, first):
    shape_of = tiles[0].shape
    index = iota(shape_of, 0)
    for base in range(0, count, WIDE):
        columns = [
            jnp.broadcast_to(tiles[0][:, first + base + a : first + base + a + 1], shape_of) for a in range(WIDE)
        ]
        rows = [[tile[base + a : base + a + 1] for tile in tiles] for a in range(WIDE)]
        factors = []
        done = []
        for a in range(WIDE):
            pivot = columns[a][base + a : base + a + 1]
            inverse = 1.0 / pivot
            for c in range(a + 1, WIDE):
                lower = columns[a][base + c : base + c + 1] * inverse
                upper = columns[c][base + a : base + a + 1] * inverse
                rows[c] = [row - lower * top for row, top in zip(rows[c], rows[a])]
                columns[c] = columns[c] - columns[a] * upper
            factors.append(jnp.where(index >= base + WIDE, columns[a] * inverse, 0.0))
            root = jnp.sqrt(pivot)
            done.append([row / root for row in rows[a]])
        tiles = list(tiles)
        for i in range(len(tiles)):
            tile = tiles[i]
            for a in range(WIDE):
                tile = tile - factors[a] * rows[a][i]
            for a in range(WIDE):
                tile = jnp.where(index == base + a, done[a][i], tile)
            tiles[i] = tile
    return tiles


def pad_lanes(a, width=EDGE):
    return jnp.concatenate([a, jnp.zeros((a.shape[0], width - a.shape[1]), F32)], axis=1)


def inverse_factor(square):
    both = pad_lanes(jnp.concatenate([square, eye(BLK, F32)], axis=1))
    return eliminate([both], BLK, 0)[0][:, BLK : 2 * BLK]


def first_solve_body(
    nodes, got_ref, all_ref, scale_ref, first_ref, send_ref, own_ref, next_ref, gram_ref, inv_ref
):
    got = got_ref[...]
    mine = got[2 * BLK :]
    low = jnp.concatenate(
        [got[:BLK], pltpu.roll(mine, BLK, 1), pltpu.roll(mine, EDGE - BLK, 1), got[BLK : 2 * BLK]], axis=0
    )
    row, lane = iota((EDGE, EDGE), 0), iota((EDGE, EDGE), 1)
    inner_row = (row >= BLK) & (row < 3 * BLK)
    inner_lane = (lane >= BLK) & (lane < 3 * BLK)
    gram = jnp.where(inner_row & jnp.logical_not(inner_lane), low.T, low)
    gram_ref[...] = gram
    unit = jnp.where(row[BLK:] == lane[BLK:], 1.0, 0.0)
    lower = eliminate([gram[BLK:], unit], 3 * BLK, BLK)[1]
    lower = jnp.concatenate([jnp.zeros((BLK, EDGE), F32), lower], axis=0)
    inv = dot_exact(lower.T, lower)
    inv_ref[...] = inv
    coef = dot_exact(gram[:BLK], inv)
    mix = jnp.where(lane[:BLK] < BLK, jnp.where(row[:BLK] == lane[:BLK], 1.0, 0.0), -coef).astype(BF16)
    wide = mix.astype(F32)
    squares = dot_exact(dot_exact(wide, gram), wide, NT) / nodes
    factor = inverse_factor(squares)
    remainder = dot(mix, all_ref[...])
    new = dot_exact(factor, remainder).astype(BF16)
    first_ref[...] = new
    next_ref[...] = jnp.concatenate([new, all_ref[BLK:]], axis=0)
    spread(new, scale_ref[...], send_ref, own_ref)


def second_solve_body(nodes, got_ref, image_ref, basis_ref, gram_ref, inv_ref, second_ref):
    got = got_ref[...]
    cross, fresh = got[:BLK], got[BLK : 2 * BLK]
    square = jnp.concatenate([got[2 * BLK :, BLK * i : BLK * (i + 1)] for i in range(4)], axis=0)
    row, lane = iota((EDGE, EDGE), 0), iota((EDGE, EDGE), 1)
    inv = inv_ref[...]
    reach = dot_exact(fresh, inv)
    schur = fresh[:, :BLK] - dot_exact(reach, fresh, NT)
    lower = inverse_factor(schur)
    newest = dot_exact(dot_exact(cross[:, :BLK] - dot_exact(cross, reach, NT), lower, NT), lower)
    older = dot_exact(cross, inv) - dot_exact(newest, reach)
    coef = jnp.where(lane[:BLK] < BLK, pad_lanes(newest), older).astype(BF16)
    wide = coef.astype(F32)
    full = jnp.concatenate([fresh, jnp.zeros((3 * BLK, EDGE), F32)], axis=0)
    gram = jnp.where(row < BLK, full, jnp.where(lane < BLK, full.T, gram_ref[...]))
    mixed = dot_exact(wide, cross, NT)
    squares = (square - mixed - mixed.T + dot_exact(dot_exact(wide, gram), wide, NT)) / nodes
    factor = inverse_factor(squares)
    remainder = image_ref[...].astype(F32) - dot(coef, basis_ref[...])
    second_ref[...] = dot_exact(factor, remainder).astype(BF16)


def per_device(tiles, tile_rows, tile_cols, node_level, level_scale, stored_basis, start_block):
    tile_stack = tiles.reshape(tiles.shape[2:])
    side = lax.axis_size("row")
    held = stored_basis.shape[0]
    nodes = held * side * lax.axis_size("col")
    pieces = held // EDGE
    me = lax.axis_index("col").reshape(1)
    send_shape = shape((side, pieces, BLK, EDGE), BF16)
    own_shape = shape((pieces, BLK, EDGE), BF16)

    def product(send, own):
        col_blk = arrive(lax.all_to_all(send, "row", 0, 0).reshape(-1, BLK, EDGE))
        near, far = gather_col(own)
        bwd, keep, away = tile_pass(pieces, me, tile_rows, tile_cols, tile_stack, col_blk, near, far)
        bwd = lax.all_to_all(bwd.reshape(send.shape), "row", 0, 0)
        keep, fwd = scatter_col(keep, away)
        return keep, fwd, bwd

    send, own, scale, basis = prep(
        send_shape,
        own_shape,
        start_block.T,
        stored_basis.T,
        node_level.reshape(1, -1),
        level_scale.reshape(1, -1),
    )
    parts = product(send, own)
    every, pay = call(
        first_image_body,
        (shape((EDGE, held), BF16), shape((3 * BLK, EDGE), F32)),
        (*parts, own, scale, basis),
    )
    got = reduce_all(pay)
    square_shape = shape((EDGE, EDGE), F32)
    first, send, own, basis, gram, inv = call(
        lambda *refs: first_solve_body(nodes, *refs),
        (
            shape((BLK, held), BF16),
            send_shape,
            own_shape,
            shape((EDGE, held), BF16),
            square_shape,
            square_shape,
        ),
        (got, every, scale),
    )
    parts = product(send, own)
    image, pay = call(
        second_image_body,
        (shape((BLK, held), BF16), shape((2 * BLK + 8, EDGE), F32)),
        (*parts, own, scale, basis),
    )
    got = reduce_all(pay)
    second = call(
        lambda *refs: second_solve_body(nodes, *refs),
        shape((BLK, held), BF16),
        (got, image, basis, gram, inv),
    )
    return (first.T, second.T)


def solution(mesh):
    return jax.shard_map(
        per_device,
        mesh=mesh,
        in_specs=(
            P("row", "col", None, None, None),
            P("row", "col", None),
            P("row", "col", None),
            P(("row", "col")),
            P(),
            P(("row", "col"), None),
            P(("row", "col"), None),
        ),
        out_specs=(P(("row", "col"), None), P(("row", "col"), None)),
        check_vma=False,
    )
```

```python
import jax
import jax.numpy as jnp
from jax import lax
from jax.experimental import pallas as pl
from jax.experimental.pallas import tpu as pltpu
from jax.sharding import PartitionSpec as P

F32 = jnp.float32
BF16 = jnp.bfloat16
EDGE = 128
BLK = 32
CHUNK = 80
WIDE = 8
NT = (((1,), (1,)), ((), ()))
NN = (((1,), (0,)), ((), ()))
VMEM = pltpu.VMEM


def dot(a, b, dims=NN):
    return lax.dot_general(a, b, dims, preferred_element_type=F32)


def dot_exact(a, b, dims=NN):
    return lax.dot_general(
        a, b, dims, preferred_element_type=F32, precision=lax.Precision.HIGHEST
    )


def iota(shape, axis):
    return lax.broadcasted_iota(jnp.int32, shape, axis)


def eye(n, dtype):
    return jnp.where(iota((n, n), 0) == iota((n, n), 1), 1.0, 0.0).astype(dtype)


def whole(count):
    return [pl.BlockSpec(memory_space=VMEM)] * count


def call(body, out_shape, args, scratch=(), vmem=24 << 20):
    return pl.pallas_call(
        body,
        out_shape=out_shape,
        in_specs=whole(len(args)),
        out_specs=jax.tree.map(lambda _: pl.BlockSpec(memory_space=VMEM), out_shape),
        scratch_shapes=list(scratch),
        compiler_params=pltpu.CompilerParams(vmem_limit_bytes=vmem),
    )(*args)


def shape(dims, dtype):
    return jax.ShapeDtypeStruct(dims, dtype)


def spread(block, scale, send_ref, own_ref):
    for j in range(block.shape[1] // EDGE):
        lanes = slice(j * EDGE, (j + 1) * EDGE)
        piece = (scale[:, lanes] * block[:, lanes].astype(F32)).astype(BF16)
        own_ref[j] = piece
        for k in range(send_ref.shape[0]):
            send_ref[k, j] = piece


def prep_body(start_in, stored_in, level_in, levels_in, send_ref, own_ref, scale_ref, basis_ref, level_ref, levels_ref, done):
    copies = [
        pltpu.make_async_copy(src, dst, done.at[i])
        for i, (src, dst) in enumerate(
            (
                (level_in, level_ref),
                (levels_in, levels_ref),
                (start_in, basis_ref.at[2 * BLK : 3 * BLK]),
                (stored_in, basis_ref.at[0 : 2 * BLK]),
            )
        )
    ]
    for copy in copies:
        copy.start()
    for copy in copies:
        copy.wait()
    table = jnp.broadcast_to(levels_ref[...], (EDGE, EDGE)).T
    for j in range(level_ref.shape[1] // EDGE):
        lanes = slice(j * EDGE, (j + 1) * EDGE)
        member = level_ref[:, lanes] == iota((EDGE, EDGE), 0)
        scale_ref[:, lanes] = jnp.sum(jnp.where(member, table, 0.0), axis=0, keepdims=True)
    spread(basis_ref[2 * BLK :], scale_ref[...], send_ref, own_ref)


def prep(send_shape, own_shape, start, stored, level, levels):
    held = start.shape[1]
    outs = (send_shape, own_shape, shape((1, held), F32), shape((3 * BLK, held), BF16))
    return pl.pallas_call(
        prep_body,
        out_shape=outs,
        in_specs=[pl.BlockSpec(memory_space=pltpu.HBM)] * 4,
        out_specs=tuple(whole(4)),
        scratch_shapes=[
            pltpu.VMEM(level.shape, jnp.int32),
            pltpu.VMEM(levels.shape, F32),
            pltpu.SemaphoreType.DMA((4,)),
        ],
        compiler_params=pltpu.CompilerParams(vmem_limit_bytes=58 << 20),
    )(start, stored, level, levels)


def pair_rows(first, second):
    none = jnp.zeros_like(first)
    return jnp.concatenate(
        [jnp.concatenate([first, none], axis=1), jnp.concatenate([none, second], axis=1)], axis=0
    )


def tile_body(
    pieces, me_in, rows_in, cols_in, tiles_ref, col_in, near_in, far_in, bwd_out, keep_out, away_out,
    me_ref, rows_ref, cols_ref, col_blk, row_blk, fwd_acc, bwd_acc, bwd_ref, keep_ref, away_ref, held, done, moved,
):
    chunks = held.shape[0]
    half = near_in.shape[0]

    def copy(i):
        part = tiles_ref.at[pl.ds(i * CHUNK, CHUNK)]
        return pltpu.make_async_copy(part, held.at[i], done.at[i])

    ins = [
        pltpu.make_async_copy(src, dst, moved.at[i])
        for i, (src, dst) in enumerate(
            (
                (col_in, col_blk),
                (near_in, row_blk.at[0:half]),
                (far_in, row_blk.at[half : 2 * half]),
                (me_in, me_ref),
                (rows_in, rows_ref),
                (cols_in, cols_ref),
            )
        )
    ]
    outs = [
        pltpu.make_async_copy(src, dst, moved.at[6 + i])
        for i, (src, dst) in enumerate(((bwd_ref, bwd_out), (keep_ref, keep_out), (away_ref, away_out)))
    ]
    copy(0).start()
    for move in ins:
        move.start()
    for i in range(1, chunks):
        copy(i).start()
    fwd_acc[...] = jnp.zeros_like(fwd_acc)
    bwd_acc[...] = jnp.zeros_like(bwd_acc)
    for move in ins:
        move.wait()
    me = me_ref[0]

    def place(row):
        apart = (row // pieces) ^ me
        return ((apart & 1) * 8 + (apart >> 1)) * pieces + (row & (pieces - 1))

    def body(i, carry):
        copy(i).wait()
        for t in range(0, CHUNK, 2):
            r = [place(rows_ref[0, 0, i * CHUNK + t + n]) for n in range(2)]
            c = [cols_ref[0, 0, i * CHUNK + t + n] for n in range(2)]
            one, two = held[i, t], held[i, t + 1]
            terms = dot(pair_rows(col_blk[c[0]], col_blk[c[1]]), jnp.concatenate([one, two], axis=1), NT)
            fwd_acc[r[0]] += terms[:BLK]
            fwd_acc[r[1]] += terms[BLK:]
            terms = dot(pair_rows(row_blk[r[0]], row_blk[r[1]]), jnp.concatenate([one, two], axis=0))
            bwd_acc[c[0]] += terms[:BLK]
            bwd_acc[c[1]] += terms[BLK:]
        return carry

    lax.fori_loop(0, chunks, body, 0)
    bwd_ref[...] = bwd_acc[...].astype(BF16)
    outs[0].start()
    away_ref[...] = fwd_acc[half:].astype(BF16)
    outs[2].start()
    keep_ref[...] = fwd_acc[:half].astype(BF16)
    outs[1].start()
    for move in outs:
        move.wait()


def tile_pass(pieces, me, rows, cols, tiles, col_blk, near, far):
    count = tiles.shape[0]
    half = near.shape
    acc = col_blk.shape
    return pl.pallas_call(
        lambda *refs: tile_body(pieces, *refs),
        out_shape=(shape(acc, BF16), shape(half, BF16), shape(half, BF16)),
        in_specs=[pl.BlockSpec(memory_space=pl.ANY)] * 3 + [pl.BlockSpec(memory_space=pltpu.HBM)] + [pl.BlockSpec(memory_space=pl.ANY)] * 3,
        out_specs=tuple([pl.BlockSpec(memory_space=pl.ANY)] * 3),
        scratch_shapes=[
            pltpu.SMEM(me.shape, jnp.int32),
            pltpu.SMEM(rows.shape, jnp.int32),
            pltpu.SMEM(cols.shape, jnp.int32),
            pltpu.VMEM(acc, BF16),
            pltpu.VMEM(acc, BF16),
            pltpu.VMEM(acc, F32),
            pltpu.VMEM(acc, F32),
            pltpu.VMEM(acc, BF16),
            pltpu.VMEM(half, BF16),
            pltpu.VMEM(half, BF16),
            pltpu.VMEM((count // CHUNK, CHUNK, EDGE, EDGE), BF16),
            pltpu.SemaphoreType.DMA((count // CHUNK,)),
            pltpu.SemaphoreType.DMA((9,)),
        ],
        cost_estimate=pl.CostEstimate(flops=8_000_000_000, bytes_accessed=14_000_000, transcendentals=0),
        compiler_params=pltpu.CompilerParams(vmem_limit_bytes=51 << 20),
    )(me, rows, cols, tiles, col_blk, near, far)


def keep_body(in_ref, out_ref):
    pass


def arrive(a):
    return pl.pallas_call(
        keep_body,
        out_shape=shape(a.shape, a.dtype),
        in_specs=[pl.BlockSpec(memory_space=pl.ANY)],
        out_specs=pl.BlockSpec(memory_space=pl.ANY),
        input_output_aliases={0: 0},
        cost_estimate=pl.CostEstimate(flops=40_000_000_000, bytes_accessed=1_000_000, transcendentals=0),
        compiler_params=pltpu.CompilerParams(vmem_limit_bytes=1 << 20),
    )(a)


def swap(a, mask):
    return lax.ppermute(a, "col", [(i, i ^ mask) for i in range(lax.axis_size("col"))])


def gather_col(own):
    two = jnp.concatenate([own, swap(own, 2)], axis=0)
    eight = jnp.concatenate([two] + [swap(two, 4 * j) for j in range(1, 4)], axis=0)
    return (eight, swap(eight, 1))


def halve_body(parts, *refs):
    ins, outs = refs[: -1 - parts], refs[-1 - parts :]
    total = ins[0][...].astype(F32)
    for ref in ins[1:]:
        total = total + ref[...].astype(F32)
    size = total.shape[0] // (1 + parts)
    for i, ref in enumerate(outs):
        ref[...] = total[i * size : (i + 1) * size].astype(ref.dtype)


def halve(parts, keep, *arrived):
    piece = (keep.shape[0] // (1 + parts),) + keep.shape[1:]
    outs = (shape(piece, F32),) + (shape(piece, BF16),) * parts
    return call(lambda *refs: halve_body(parts, *refs), outs, (keep, *arrived))


def scatter_col(keep, send):
    keep, *sends = halve(3, keep, swap(send, 1))
    arrived = [swap(send, 4 * (j + 1)) for j, send in enumerate(sends)]
    keep, send = halve(1, keep, *arrived)
    return keep, swap(send, 2)


def image_of(keep_ref, fwd_ref, bwd_ref, own_ref, scale_ref):
    pieces = []
    for j in range(own_ref.shape[0]):
        total = own_ref[j].astype(F32) + keep_ref[j] + fwd_ref[j].astype(F32)
        for k in range(bwd_ref.shape[0]):
            total += bwd_ref[k, j].astype(F32)
        pieces.append((scale_ref[:, j * EDGE : (j + 1) * EDGE] * total).astype(BF16))
    return jnp.concatenate(pieces, axis=1)


def first_image_body(keep_ref, fwd_ref, bwd_ref, own_ref, scale_ref, basis_ref, all_ref, pay_ref):
    image = image_of(keep_ref, fwd_ref, bwd_ref, own_ref, scale_ref)
    basis = basis_ref[...]
    every = jnp.concatenate([image, basis], axis=0)
    all_ref[...] = every
    gram = dot(every, every, NT)
    half = EDGE // 2
    row, lane = iota((half, EDGE), 0), iota((half, EDGE), 1)
    turned = pltpu.roll(gram[half:], half, 1)
    pay_ref[0:half] = jnp.where((lane >= half) | (lane <= row), gram[:half], turned)
    diagonal = jnp.sum(jnp.where(lane == row, turned, 0.0), axis=0, keepdims=True)
    pay_ref[half:] = jnp.broadcast_to(diagonal, (8, EDGE))


def unfold(pay):
    half = EDGE // 2
    row, lane = iota((half, EDGE), 0), iota((half, EDGE), 1)
    part = pay[:half]
    first = jnp.where((lane >= half) | (lane < row), part, 0.0)
    second = pltpu.roll(jnp.where((lane < half) & (lane > row), part, 0.0), half, 1)
    off = jnp.concatenate([first, second], axis=0)
    ends = jnp.broadcast_to(pltpu.roll(pay[half : half + 8], half, 1)[:1], (half, EDGE))
    diagonal = jnp.concatenate(
        [jnp.where(lane == row, part, 0.0), jnp.where(lane == row + half, ends, 0.0)], axis=0
    )
    return off + off.T + diagonal


def second_image_body(keep_ref, fwd_ref, bwd_ref, own_ref, scale_ref, basis_ref, image_ref, pay_ref):
    image = image_of(keep_ref, fwd_ref, bwd_ref, own_ref, scale_ref)
    image_ref[...] = image
    basis = basis_ref[...]
    square = dot(image, image, NT)
    pay_ref[0:BLK] = dot(image, basis, NT)
    pay_ref[BLK : 2 * BLK] = dot(basis[:BLK], basis, NT)
    pay_ref[2 * BLK :] = jnp.concatenate([square[8 * i : 8 * i + 8] for i in range(4)], axis=1)


def sum_body(*refs):
    parts = [ref[...] for ref in refs[:-1]]
    while len(parts) > 1:
        parts = [one + other for one, other in zip(parts[::2], parts[1::2])]
    refs[-1][...] = parts[0]


def reduce_all(pay):
    count = lax.axis_size("row") * lax.axis_size("col")
    for masks in ORDER:
        others = [lax.ppermute(pay, ("row", "col"), [(i, i ^ mask) for i in range(count)]) for mask in masks]
        pay = call(sum_body, shape(pay.shape, F32), (pay, *others))
    return pay


ORDER = ((1, 2, 3), (16, 32, 48), (64, 128, 192), (4, 8, 12))


def eliminate(tiles, count, first):
    shape_of = tiles[0].shape
    index = iota(shape_of, 0)
    for base in range(0, count, WIDE):
        columns = [
            jnp.broadcast_to(tiles[0][:, first + base + a : first + base + a + 1], shape_of) for a in range(WIDE)
        ]
        rows = [[tile[base + a : base + a + 1] for tile in tiles] for a in range(WIDE)]
        factors = []
        done = []
        for a in range(WIDE):
            pivot = columns[a][base + a : base + a + 1]
            inverse = 1.0 / pivot
            for c in range(a + 1, WIDE):
                lower = columns[a][base + c : base + c + 1] * inverse
                upper = columns[c][base + a : base + a + 1] * inverse
                rows[c] = [row - lower * top for row, top in zip(rows[c], rows[a])]
                columns[c] = columns[c] - columns[a] * upper
            factors.append(jnp.where(index >= base + WIDE, columns[a] * inverse, 0.0))
            root = jnp.sqrt(pivot)
            done.append([row / root for row in rows[a]])
        tiles = list(tiles)
        for i in range(len(tiles)):
            tile = tiles[i]
            for a in range(WIDE):
                tile = tile - factors[a] * rows[a][i]
            for a in range(WIDE):
                tile = jnp.where(index == base + a, done[a][i], tile)
            tiles[i] = tile
    return tiles


def pad_lanes(a, width=EDGE):
    return jnp.concatenate([a, jnp.zeros((a.shape[0], width - a.shape[1]), F32)], axis=1)


def inverse_factor(square):
    both = pad_lanes(jnp.concatenate([square, eye(BLK, F32)], axis=1))
    return eliminate([both], BLK, 0)[0][:, BLK : 2 * BLK]


def first_solve_body(
    nodes, got_ref, all_ref, scale_ref, first_ref, send_ref, own_ref, next_ref, gram_ref, inv_ref
):
    row, lane = iota((EDGE, EDGE), 0), iota((EDGE, EDGE), 1)
    gram = unfold(got_ref[...])
    gram_ref[...] = gram
    unit = jnp.where(row[BLK:] == lane[BLK:], 1.0, 0.0)
    lower = eliminate([gram[BLK:], unit], 3 * BLK, BLK)[1]
    lower = jnp.concatenate([jnp.zeros((BLK, EDGE), F32), lower], axis=0)
    inv = dot_exact(lower.T, lower)
    inv_ref[...] = inv
    coef = dot_exact(gram[:BLK], inv)
    mix = jnp.where(lane[:BLK] < BLK, jnp.where(row[:BLK] == lane[:BLK], 1.0, 0.0), -coef).astype(BF16)
    wide = mix.astype(F32)
    squares = dot_exact(dot_exact(wide, gram), wide, NT) / nodes
    factor = inverse_factor(squares)
    remainder = dot(mix, all_ref[...])
    new = dot_exact(factor, remainder).astype(BF16)
    first_ref[...] = new
    next_ref[...] = jnp.concatenate([new, all_ref[BLK:]], axis=0)
    spread(new, scale_ref[...], send_ref, own_ref)


def second_solve_body(nodes, got_ref, image_ref, basis_ref, gram_ref, inv_ref, second_ref):
    got = got_ref[...]
    cross, fresh = got[:BLK], got[BLK : 2 * BLK]
    square = jnp.concatenate([got[2 * BLK :, BLK * i : BLK * (i + 1)] for i in range(4)], axis=0)
    row, lane = iota((EDGE, EDGE), 0), iota((EDGE, EDGE), 1)
    inv = inv_ref[...]
    reach = dot_exact(fresh, inv)
    schur = fresh[:, :BLK] - dot_exact(reach, fresh, NT)
    lower = inverse_factor(schur)
    newest = dot_exact(dot_exact(cross[:, :BLK] - dot_exact(cross, reach, NT), lower, NT), lower)
    older = dot_exact(cross, inv) - dot_exact(newest, reach)
    coef = jnp.where(lane[:BLK] < BLK, pad_lanes(newest), older).astype(BF16)
    wide = coef.astype(F32)
    full = jnp.concatenate([fresh, jnp.zeros((3 * BLK, EDGE), F32)], axis=0)
    gram = jnp.where(row < BLK, full, jnp.where(lane < BLK, full.T, gram_ref[...]))
    mixed = dot_exact(wide, cross, NT)
    squares = (square - mixed - mixed.T + dot_exact(dot_exact(wide, gram), wide, NT)) / nodes
    factor = inverse_factor(squares)
    remainder = image_ref[...].astype(F32) - dot(coef, basis_ref[...])
    second_ref[...] = dot_exact(factor, remainder).astype(BF16)


def per_device(tiles, tile_rows, tile_cols, node_level, level_scale, stored_basis, start_block):
    tile_stack = tiles.reshape(tiles.shape[2:])
    side = lax.axis_size("row")
    held = stored_basis.shape[0]
    nodes = held * side * lax.axis_size("col")
    pieces = held // EDGE
    me = lax.axis_index("col").reshape(1)
    send_shape = shape((side, pieces, BLK, EDGE), BF16)
    own_shape = shape((pieces, BLK, EDGE), BF16)

    def product(send, own):
        col_blk = arrive(lax.all_to_all(send, "row", 0, 0).reshape(-1, BLK, EDGE))
        near, far = gather_col(own)
        bwd, keep, away = tile_pass(pieces, me, tile_rows, tile_cols, tile_stack, col_blk, near, far)
        bwd = lax.all_to_all(bwd.reshape(send.shape), "row", 0, 0)
        keep, fwd = scatter_col(keep, away)
        return keep, fwd, bwd

    send, own, scale, basis = prep(
        send_shape,
        own_shape,
        start_block.T,
        stored_basis.T,
        node_level.reshape(1, -1),
        level_scale.reshape(1, -1),
    )
    parts = product(send, own)
    every, pay = call(
        first_image_body,
        (shape((EDGE, held), BF16), shape((2 * BLK + 8, EDGE), F32)),
        (*parts, own, scale, basis),
    )
    got = reduce_all(pay)
    square_shape = shape((EDGE, EDGE), F32)
    first, send, own, basis, gram, inv = call(
        lambda *refs: first_solve_body(nodes, *refs),
        (
            shape((BLK, held), BF16),
            send_shape,
            own_shape,
            shape((EDGE, held), BF16),
            square_shape,
            square_shape,
        ),
        (got, every, scale),
    )
    parts = product(send, own)
    image, pay = call(
        second_image_body,
        (shape((BLK, held), BF16), shape((2 * BLK + 8, EDGE), F32)),
        (*parts, own, scale, basis),
    )
    got = reduce_all(pay)
    second = call(
        lambda *refs: second_solve_body(nodes, *refs),
        shape((BLK, held), BF16),
        (got, image, basis, gram, inv),
    )
    return (first.T, second.T)


def solution(mesh):
    return jax.shard_map(
        per_device,
        mesh=mesh,
        in_specs=(
            P("row", "col", None, None, None),
            P("row", "col", None),
            P("row", "col", None),
            P(("row", "col")),
            P(),
            P(("row", "col"), None),
            P(("row", "col"), None),
        ),
        out_specs=(P(("row", "col"), None), P(("row", "col"), None)),
        check_vma=False,
    )
```

```python
import jax
import jax.numpy as jnp
from jax import lax
from jax.experimental import pallas as pl
from jax.experimental.pallas import tpu as pltpu
from jax.sharding import PartitionSpec as P

F32 = jnp.float32
BF16 = jnp.bfloat16
EDGE = 128
BLK = 32
CHUNK = 80
WIDE = 8
NT = (((1,), (1,)), ((), ()))
NN = (((1,), (0,)), ((), ()))
VMEM = pltpu.VMEM


def dot(a, b, dims=NN):
    return lax.dot_general(a, b, dims, preferred_element_type=F32)


def dot_exact(a, b, dims=NN):
    return lax.dot_general(
        a, b, dims, preferred_element_type=F32, precision=lax.Precision.HIGHEST
    )


def iota(shape, axis):
    return lax.broadcasted_iota(jnp.int32, shape, axis)


def eye(n, dtype):
    return jnp.where(iota((n, n), 0) == iota((n, n), 1), 1.0, 0.0).astype(dtype)


def whole(count):
    return [pl.BlockSpec(memory_space=VMEM)] * count


def call(body, out_shape, args, scratch=(), vmem=24 << 20):
    return pl.pallas_call(
        body,
        out_shape=out_shape,
        in_specs=whole(len(args)),
        out_specs=jax.tree.map(lambda _: pl.BlockSpec(memory_space=VMEM), out_shape),
        scratch_shapes=list(scratch),
        compiler_params=pltpu.CompilerParams(vmem_limit_bytes=vmem),
    )(*args)


def shape(dims, dtype):
    return jax.ShapeDtypeStruct(dims, dtype)


def spread(block, scale, send_ref, own_ref):
    for j in range(block.shape[1] // EDGE):
        lanes = slice(j * EDGE, (j + 1) * EDGE)
        piece = (scale[:, lanes] * block[:, lanes].astype(F32)).astype(BF16)
        own_ref[j] = piece
        for k in range(send_ref.shape[0]):
            send_ref[k, j] = piece


def prep_body(start_in, stored_in, level_in, levels_in, send_ref, own_ref, scale_ref, basis_ref, level_ref, levels_ref, done):
    copies = [
        pltpu.make_async_copy(src, dst, done.at[i])
        for i, (src, dst) in enumerate(
            (
                (level_in, level_ref),
                (levels_in, levels_ref),
                (start_in, basis_ref.at[2 * BLK : 3 * BLK]),
                (stored_in, basis_ref.at[0 : 2 * BLK]),
            )
        )
    ]
    for copy in copies:
        copy.start()
    for copy in copies:
        copy.wait()
    table = jnp.broadcast_to(levels_ref[...], (EDGE, EDGE)).T
    for j in range(level_ref.shape[1] // EDGE):
        lanes = slice(j * EDGE, (j + 1) * EDGE)
        member = level_ref[:, lanes] == iota((EDGE, EDGE), 0)
        scale_ref[:, lanes] = jnp.sum(jnp.where(member, table, 0.0), axis=0, keepdims=True)
    spread(basis_ref[2 * BLK :], scale_ref[...], send_ref, own_ref)


def prep(send_shape, own_shape, start, stored, level, levels):
    held = start.shape[1]
    outs = (send_shape, own_shape, shape((1, held), F32), shape((3 * BLK, held), BF16))
    return pl.pallas_call(
        prep_body,
        out_shape=outs,
        in_specs=[pl.BlockSpec(memory_space=pltpu.HBM)] * 4,
        out_specs=tuple(whole(4)),
        scratch_shapes=[
            pltpu.VMEM(level.shape, jnp.int32),
            pltpu.VMEM(levels.shape, F32),
            pltpu.SemaphoreType.DMA((4,)),
        ],
        compiler_params=pltpu.CompilerParams(vmem_limit_bytes=58 << 20),
    )(start, stored, level, levels)


def pair_rows(first, second):
    none = jnp.zeros_like(first)
    return jnp.concatenate(
        [jnp.concatenate([first, none], axis=1), jnp.concatenate([none, second], axis=1)], axis=0
    )


def tile_body(
    pieces, me_in, rows_in, cols_in, tiles_ref, col_in, near_in, far_in, bwd_out, keep_out, away_out,
    me_ref, rows_ref, cols_ref, col_blk, row_blk, fwd_acc, bwd_acc, bwd_ref, keep_ref, away_ref, held, done, moved,
):
    chunks = held.shape[0]
    half = near_in.shape[0]

    def copy(i):
        part = tiles_ref.at[pl.ds(i * CHUNK, CHUNK)]
        return pltpu.make_async_copy(part, held.at[i], done.at[i])

    ins = [
        pltpu.make_async_copy(src, dst, moved.at[i])
        for i, (src, dst) in enumerate(
            (
                (col_in, col_blk),
                (near_in, row_blk.at[0:half]),
                (far_in, row_blk.at[half : 2 * half]),
                (me_in, me_ref),
                (rows_in, rows_ref),
                (cols_in, cols_ref),
            )
        )
    ]
    outs = [
        pltpu.make_async_copy(src, dst, moved.at[6 + i])
        for i, (src, dst) in enumerate(((bwd_ref, bwd_out), (keep_ref, keep_out), (away_ref, away_out)))
    ]
    copy(0).start()
    for move in ins:
        move.start()
    for i in range(1, chunks):
        copy(i).start()
    fwd_acc[...] = jnp.zeros_like(fwd_acc)
    bwd_acc[...] = jnp.zeros_like(bwd_acc)
    for move in ins:
        move.wait()
    me = me_ref[0]

    def place(row):
        apart = (row // pieces) ^ me
        return ((apart & 1) * 8 + (apart >> 1)) * pieces + (row & (pieces - 1))

    def body(i, carry):
        copy(i).wait()
        for t in range(0, CHUNK, 2):
            r = [place(rows_ref[0, 0, i * CHUNK + t + n]) for n in range(2)]
            c = [cols_ref[0, 0, i * CHUNK + t + n] for n in range(2)]
            one, two = held[i, t], held[i, t + 1]
            terms = dot(pair_rows(col_blk[c[0]], col_blk[c[1]]), jnp.concatenate([one, two], axis=1), NT)
            fwd_acc[r[0]] += terms[:BLK]
            fwd_acc[r[1]] += terms[BLK:]
            terms = dot(pair_rows(row_blk[r[0]], row_blk[r[1]]), jnp.concatenate([one, two], axis=0))
            bwd_acc[c[0]] += terms[:BLK]
            bwd_acc[c[1]] += terms[BLK:]
        return carry

    lax.fori_loop(0, chunks, body, 0)
    bwd_ref[...] = bwd_acc[...].astype(BF16)
    outs[0].start()
    away_ref[...] = fwd_acc[half:].astype(BF16)
    outs[2].start()
    keep_ref[...] = fwd_acc[:half].astype(BF16)
    outs[1].start()
    for move in outs:
        move.wait()


def tile_pass(pieces, me, rows, cols, tiles, col_blk, near, far):
    count = tiles.shape[0]
    half = near.shape
    acc = col_blk.shape
    return pl.pallas_call(
        lambda *refs: tile_body(pieces, *refs),
        out_shape=(shape(acc, BF16), shape(half, BF16), shape(half, BF16)),
        in_specs=[pl.BlockSpec(memory_space=pl.ANY)] * 3 + [pl.BlockSpec(memory_space=pltpu.HBM)] + [pl.BlockSpec(memory_space=pl.ANY)] * 3,
        out_specs=tuple([pl.BlockSpec(memory_space=pl.ANY)] * 3),
        scratch_shapes=[
            pltpu.SMEM(me.shape, jnp.int32),
            pltpu.SMEM(rows.shape, jnp.int32),
            pltpu.SMEM(cols.shape, jnp.int32),
            pltpu.VMEM(acc, BF16),
            pltpu.VMEM(acc, BF16),
            pltpu.VMEM(acc, F32),
            pltpu.VMEM(acc, F32),
            pltpu.VMEM(acc, BF16),
            pltpu.VMEM(half, BF16),
            pltpu.VMEM(half, BF16),
            pltpu.VMEM((count // CHUNK, CHUNK, EDGE, EDGE), BF16),
            pltpu.SemaphoreType.DMA((count // CHUNK,)),
            pltpu.SemaphoreType.DMA((9,)),
        ],
        cost_estimate=pl.CostEstimate(flops=8_000_000_000, bytes_accessed=14_000_000, transcendentals=0),
        compiler_params=pltpu.CompilerParams(vmem_limit_bytes=51 << 20),
    )(me, rows, cols, tiles, col_blk, near, far)


def keep_body(in_ref, out_ref):
    pass


def arrive(a):
    return pl.pallas_call(
        keep_body,
        out_shape=shape(a.shape, a.dtype),
        in_specs=[pl.BlockSpec(memory_space=pl.ANY)],
        out_specs=pl.BlockSpec(memory_space=pl.ANY),
        input_output_aliases={0: 0},
        cost_estimate=pl.CostEstimate(flops=40_000_000_000, bytes_accessed=1_000_000, transcendentals=0),
        compiler_params=pltpu.CompilerParams(vmem_limit_bytes=1 << 20),
    )(a)


def swap(a, mask):
    return lax.ppermute(a, "col", [(i, i ^ mask) for i in range(lax.axis_size("col"))])


def gather_col(own):
    two = jnp.concatenate([own, swap(own, 2)], axis=0)
    eight = jnp.concatenate([two] + [swap(two, 4 * j) for j in range(1, 4)], axis=0)
    return (eight, swap(eight, 1))


def halve_body(parts, *refs):
    ins, outs = refs[: -1 - parts], refs[-1 - parts :]
    total = ins[0][...].astype(F32)
    for ref in ins[1:]:
        total = total + ref[...].astype(F32)
    size = total.shape[0] // (1 + parts)
    for i, ref in enumerate(outs):
        ref[...] = total[i * size : (i + 1) * size].astype(ref.dtype)


def halve(parts, keep, *arrived):
    piece = (keep.shape[0] // (1 + parts),) + keep.shape[1:]
    outs = (shape(piece, F32),) + (shape(piece, BF16),) * parts
    return call(lambda *refs: halve_body(parts, *refs), outs, (keep, *arrived))


def scatter_col(keep, send):
    keep, *sends = halve(3, keep, arrive(swap(send, 1)))
    arrived = [swap(send, 4 * (j + 1)) for j, send in enumerate(sends)]
    keep, send = halve(1, keep, *arrived)
    return keep, swap(send, 2)


def image_of(keep_ref, fwd_ref, bwd_ref, own_ref, scale_ref):
    pieces = []
    for j in range(own_ref.shape[0]):
        total = own_ref[j].astype(F32) + keep_ref[j] + fwd_ref[j].astype(F32)
        for k in range(bwd_ref.shape[0]):
            total += bwd_ref[k, j].astype(F32)
        pieces.append((scale_ref[:, j * EDGE : (j + 1) * EDGE] * total).astype(BF16))
    return jnp.concatenate(pieces, axis=1)


def first_image_body(keep_ref, fwd_ref, bwd_ref, own_ref, scale_ref, basis_ref, all_ref, pay_ref):
    image = image_of(keep_ref, fwd_ref, bwd_ref, own_ref, scale_ref)
    basis = basis_ref[...]
    every = jnp.concatenate([image, basis], axis=0)
    all_ref[...] = every
    gram = dot(every, every, NT)
    half = EDGE // 2
    row, lane = iota((half, EDGE), 0), iota((half, EDGE), 1)
    turned = pltpu.roll(gram[half:], half, 1)
    pay_ref[0:half] = jnp.where((lane >= half) | (lane <= row), gram[:half], turned)
    diagonal = jnp.sum(jnp.where(lane == row, turned, 0.0), axis=0, keepdims=True)
    pay_ref[half:] = jnp.broadcast_to(diagonal, (8, EDGE))


def unfold(pay):
    half = EDGE // 2
    row, lane = iota((half, EDGE), 0), iota((half, EDGE), 1)
    part = pay[:half]
    first = jnp.where((lane >= half) | (lane < row), part, 0.0)
    second = pltpu.roll(jnp.where((lane < half) & (lane > row), part, 0.0), half, 1)
    off = jnp.concatenate([first, second], axis=0)
    ends = jnp.broadcast_to(pltpu.roll(pay[half : half + 8], half, 1)[:1], (half, EDGE))
    diagonal = jnp.concatenate(
        [jnp.where(lane == row, part, 0.0), jnp.where(lane == row + half, ends, 0.0)], axis=0
    )
    return off + off.T + diagonal


def second_image_body(keep_ref, fwd_ref, bwd_ref, own_ref, scale_ref, basis_ref, image_ref, pay_ref):
    image = image_of(keep_ref, fwd_ref, bwd_ref, own_ref, scale_ref)
    image_ref[...] = image
    basis = basis_ref[...]
    square = dot(image, image, NT)
    pay_ref[0:BLK] = dot(image, basis, NT)
    pay_ref[BLK : 2 * BLK] = dot(basis[:BLK], basis, NT)
    pay_ref[2 * BLK :] = jnp.concatenate([square[8 * i : 8 * i + 8] for i in range(4)], axis=1)


def sum_body(*refs):
    parts = [ref[...] for ref in refs[:-1]]
    while len(parts) > 1:
        parts = [one + other for one, other in zip(parts[::2], parts[1::2])]
    refs[-1][...] = parts[0]


def reduce_all(pay):
    count = lax.axis_size("row") * lax.axis_size("col")
    for masks in ORDER:
        others = [lax.ppermute(pay, ("row", "col"), [(i, i ^ mask) for i in range(count)]) for mask in masks]
        pay = call(sum_body, shape(pay.shape, F32), (pay, *others))
    return pay


ORDER = ((1, 2, 3), (16, 32, 48), (64, 128, 192), (4, 8, 12))


def eliminate(tiles, count, first):
    shape_of = tiles[0].shape
    index = iota(shape_of, 0)
    for base in range(0, count, WIDE):
        columns = [
            jnp.broadcast_to(tiles[0][:, first + base + a : first + base + a + 1], shape_of) for a in range(WIDE)
        ]
        rows = [[tile[base + a : base + a + 1] for tile in tiles] for a in range(WIDE)]
        factors = []
        done = []
        for a in range(WIDE):
            pivot = columns[a][base + a : base + a + 1]
            inverse = 1.0 / pivot
            for c in range(a + 1, WIDE):
                lower = columns[a][base + c : base + c + 1] * inverse
                upper = columns[c][base + a : base + a + 1] * inverse
                rows[c] = [row - lower * top for row, top in zip(rows[c], rows[a])]
                columns[c] = columns[c] - columns[a] * upper
            factors.append(jnp.where(index >= base + WIDE, columns[a] * inverse, 0.0))
            root = jnp.sqrt(pivot)
            done.append([row / root for row in rows[a]])
        tiles = list(tiles)
        for i in range(len(tiles)):
            tile = tiles[i]
            for a in range(WIDE):
                tile = tile - factors[a] * rows[a][i]
            for a in range(WIDE):
                tile = jnp.where(index == base + a, done[a][i], tile)
            tiles[i] = tile
    return tiles


def pad_lanes(a, width=EDGE):
    return jnp.concatenate([a, jnp.zeros((a.shape[0], width - a.shape[1]), F32)], axis=1)


def inverse_factor(square):
    both = pad_lanes(jnp.concatenate([square, eye(BLK, F32)], axis=1))
    return eliminate([both], BLK, 0)[0][:, BLK : 2 * BLK]


def first_solve_body(
    nodes, got_ref, all_ref, scale_ref, first_ref, send_ref, own_ref, next_ref, gram_ref, inv_ref
):
    row, lane = iota((EDGE, EDGE), 0), iota((EDGE, EDGE), 1)
    gram = unfold(got_ref[...])
    gram_ref[...] = gram
    unit = jnp.where(row[BLK:] == lane[BLK:], 1.0, 0.0)
    lower = eliminate([gram[BLK:], unit], 3 * BLK, BLK)[1]
    lower = jnp.concatenate([jnp.zeros((BLK, EDGE), F32), lower], axis=0)
    inv = dot_exact(lower.T, lower)
    inv_ref[...] = inv
    coef = dot_exact(gram[:BLK], inv)
    mix = jnp.where(lane[:BLK] < BLK, jnp.where(row[:BLK] == lane[:BLK], 1.0, 0.0), -coef).astype(BF16)
    wide = mix.astype(F32)
    squares = dot_exact(dot_exact(wide, gram), wide, NT) / nodes
    factor = inverse_factor(squares)
    remainder = dot(mix, all_ref[...])
    new = dot_exact(factor, remainder).astype(BF16)
    first_ref[...] = new
    next_ref[...] = jnp.concatenate([new, all_ref[BLK:]], axis=0)
    spread(new, scale_ref[...], send_ref, own_ref)


def second_solve_body(nodes, got_ref, image_ref, basis_ref, gram_ref, inv_ref, second_ref):
    got = got_ref[...]
    cross, fresh = got[:BLK], got[BLK : 2 * BLK]
    square = jnp.concatenate([got[2 * BLK :, BLK * i : BLK * (i + 1)] for i in range(4)], axis=0)
    row, lane = iota((EDGE, EDGE), 0), iota((EDGE, EDGE), 1)
    inv = inv_ref[...]
    reach = dot_exact(fresh, inv)
    schur = fresh[:, :BLK] - dot_exact(reach, fresh, NT)
    lower = inverse_factor(schur)
    newest = dot_exact(dot_exact(cross[:, :BLK] - dot_exact(cross, reach, NT), lower, NT), lower)
    older = dot_exact(cross, inv) - dot_exact(newest, reach)
    coef = jnp.where(lane[:BLK] < BLK, pad_lanes(newest), older).astype(BF16)
    wide = coef.astype(F32)
    full = jnp.concatenate([fresh, jnp.zeros((3 * BLK, EDGE), F32)], axis=0)
    gram = jnp.where(row < BLK, full, jnp.where(lane < BLK, full.T, gram_ref[...]))
    mixed = dot_exact(wide, cross, NT)
    squares = (square - mixed - mixed.T + dot_exact(dot_exact(wide, gram), wide, NT)) / nodes
    factor = inverse_factor(squares)
    remainder = image_ref[...].astype(F32) - dot(coef, basis_ref[...])
    second_ref[...] = dot_exact(factor, remainder).astype(BF16)


def per_device(tiles, tile_rows, tile_cols, node_level, level_scale, stored_basis, start_block):
    tile_stack = tiles.reshape(tiles.shape[2:])
    side = lax.axis_size("row")
    held = stored_basis.shape[0]
    nodes = held * side * lax.axis_size("col")
    pieces = held // EDGE
    me = lax.axis_index("col").reshape(1)
    send_shape = shape((side, pieces, BLK, EDGE), BF16)
    own_shape = shape((pieces, BLK, EDGE), BF16)

    def product(send, own):
        col_blk = arrive(lax.all_to_all(send, "row", 0, 0).reshape(-1, BLK, EDGE))
        near, far = gather_col(own)
        bwd, keep, away = tile_pass(pieces, me, tile_rows, tile_cols, tile_stack, col_blk, near, far)
        bwd = lax.all_to_all(bwd.reshape(send.shape), "row", 0, 0)
        keep, fwd = scatter_col(keep, away)
        return keep, fwd, bwd

    send, own, scale, basis = prep(
        send_shape,
        own_shape,
        start_block.T,
        stored_basis.T,
        node_level.reshape(1, -1),
        level_scale.reshape(1, -1),
    )
    parts = product(send, own)
    every, pay = call(
        first_image_body,
        (shape((EDGE, held), BF16), shape((2 * BLK + 8, EDGE), F32)),
        (*parts, own, scale, basis),
    )
    got = reduce_all(pay)
    square_shape = shape((EDGE, EDGE), F32)
    first, send, own, basis, gram, inv = call(
        lambda *refs: first_solve_body(nodes, *refs),
        (
            shape((BLK, held), BF16),
            send_shape,
            own_shape,
            shape((EDGE, held), BF16),
            square_shape,
            square_shape,
        ),
        (got, every, scale),
    )
    parts = product(send, own)
    image, pay = call(
        second_image_body,
        (shape((BLK, held), BF16), shape((2 * BLK + 8, EDGE), F32)),
        (*parts, own, scale, basis),
    )
    got = reduce_all(pay)
    second = call(
        lambda *refs: second_solve_body(nodes, *refs),
        shape((BLK, held), BF16),
        (got, image, basis, gram, inv),
    )
    return (first.T, second.T)


def solution(mesh):
    return jax.shard_map(
        per_device,
        mesh=mesh,
        in_specs=(
            P("row", "col", None, None, None),
            P("row", "col", None),
            P("row", "col", None),
            P(("row", "col")),
            P(),
            P(("row", "col"), None),
            P(("row", "col"), None),
        ),
        out_specs=(P(("row", "col"), None), P(("row", "col"), None)),
        check_vma=False,
    )
```
